256 devices in a mesh: dp: 16 (over x_hi, y, core), shard: 16 (over x_lo, z).
Axes of the slice: x: 4 (x_hi: 2, x_lo: 2; x = x_hi * 2 + x_lo), y: 4, z: 8, core: 2. Of those that a mesh axis runs over, the one named last changes fastest.
Arguments:
- tokens: bfloat16 [40960, 16384], P(('dp', 'shard')), may hold values from -24 to 24
- rotated_key_gradient: bfloat16 [40960, 512], P(('dp', 'shard')), may hold values from -6 to 6
- document_numbers: int32 [16, 2560], P('dp', 'shard'), may hold values from 0 to 15, never falling along the last dimension, each value on 1 to 640 neighbouring positions
- frozen_base_levels: bfloat16 [16384, 512], P('shard'), may hold values from -1 to 1
- first_level_scales: bfloat16 [256, 512], P('shard'), may hold values from 0.5 to 2
- second_level_scales: float32 [1, 512], replicated, may hold values from 0.01 to 0.03
- adapter_down_matrix: bfloat16 [16384, 64], P('shard'), may hold values from -0.046875 to 0.046875
- adapter_up_matrix: bfloat16 [64, 512], replicated, may hold values from -0.75 to 0.75
Outputs:
- grad_tokens: bfloat16 [40960, 16384], P(('dp', 'shard'))
- grad_down: float32 [16384, 64], P('shard')
- grad_up: float32 [64, 512], replicated
The draws below stay inside these ranges and needn't reach their ends.
Inputs may be any that keep to these rules, and one draw needn't show every extreme that they name: `document_numbers`: along each packed sequence the ids never fall; every id of 0 to 15 appears, each on at most 640 consecutive places, and some id on exactly that many.
All inputs are finite; a program needn't handle non-finite values.
Results may differ from the reference program's by a relative error of at most 0.0056.
Values may be sent and summed in bfloat16 or wider, within the bound.
No kernel may reach another device: no remote copies, remote signals or barrier semaphores. Data moves between devices by JAX's collectives and lax.ppermute only.
A program may use at most 128 MiB of HBM per device.

```python
import math
import jax
import jax.numpy as jnp
import numpy as np
from jax import lax

MODEL_WIDTH = 16384
HEAD = 128
ADAPTER_RANK = 64
BLOCK = 64
SGROUP = 256
SEGS = 16
KEY_FEATURES = 512
LEN = 2560
TOKENS = 40960
N_DP = 16


def with_spikes(array, own_key, source, target, parts, factor):
    owner, partner = [(jnp.arange(array.shape[axis_at]) // (array.shape[axis_at] // parts)).reshape([-1 if axis == axis_at else 1 for axis in range(array.ndim)]) for axis_at in (source, target)]
    chosen = jax.random.permutation(own_key, parts)[partner]
    strong = (owner == chosen) | (owner == (partner + parts // 2) % parts)
    return jnp.where(strong, factor * array, array)


def block_levels(own_key, dims, pieces, smallest, top_value):
    def one(dim, blocks):
        heights = jax.random.uniform(jax.random.fold_in(jax.random.fold_in(own_key, 6), dim), (blocks,), jnp.float32, smallest / len(pieces), top_value / len(pieces))
        return jnp.repeat(jnp.exp(heights), dims[dim] // blocks).reshape((-1,) + (1,) * (len(dims) - dim - 1))

    factor_of = one(*pieces[0])
    for cut in pieces[1:]:
        factor_of = factor_of * one(*cut)
    return factor_of


def profile(count, total, most, skew):
    portions = [(1 << 20) // math.isqrt(standing ** skew) + 1 for standing in range(2, count + 1)]
    spare, given = total - most - (count - 1), [1] * (count - 1)
    while spare > 0:
        free = [i for i in range(count - 1) if given[i] < most]
        whole, left = sum([portions[i] for i in free]), spare
        for i in free:
            extra = min(most - given[i], max(1, left * portions[i] // whole), spare)
            given[i] = given[i] + extra
            spare = spare - extra
    return np.array([most] + given)


def ragged_sizes(rng, amount, total, most, slope):
    if amount == 2:
        one = jax.random.randint(rng, (), max(1, total - most), min(most, total - 1) + 1)
        return jnp.stack([one, total - one])
    tallies = jnp.asarray(profile(amount, total, most, slope), jnp.int32)
    pairs = (amount - 1) // 2
    donor, receiver = tallies[1:1 + 2 * pairs:2], tallies[2:2 + 2 * pairs:2]
    margin = jnp.minimum(donor - 1, most - receiver)
    moved = jax.random.randint(jax.random.fold_in(rng, 1), (pairs,), 0, 1 << 20) % (margin + 1)
    tallies = tallies.at[1:1 + 2 * pairs:2].set(donor - moved).at[2:2 + 2 * pairs:2].set(receiver + moved)
    return tallies[jax.random.permutation(jax.random.fold_in(rng, 2), amount)]


def bell_draw(key, shape, spread, most, cuts=(), kind=jnp.bfloat16):
    result = spread * jax.random.normal(key, shape, jnp.float32)
    if cuts:
        result = result * block_levels(key, shape, cuts, -0.22, 0.18)
    return jnp.clip(result, -most, most).astype(kind)


def bell_draw_with(own_key, dims, scale, limit, shards, heavy, held_as=jnp.bfloat16):
    array = scale * jax.random.normal(own_key, dims, jnp.float32)
    if shards:
        array = array * block_levels(own_key, dims, shards, -0.22, 0.18)
    return jnp.clip(with_spikes(array, jax.random.fold_in(own_key, 3), *heavy), -limit, limit).astype(held_as)


def setup_inputs(seed: int = 0) -> dict:
    key_of = jax.random.split(jax.random.key(seed), 9)
    return {
        "tokens": bell_draw_with(key_of[0], (TOKENS, MODEL_WIDTH), 1.0, 24.0, ((0, 256),), (0, 1, 256, 6.0)),
        "rotated_key_gradient": bell_draw(key_of[1], (TOKENS, KEY_FEATURES), 1.0, 6.0, ((0, 256),)),
        "document_numbers": jax.vmap(lambda own: jnp.searchsorted(jnp.cumsum(ragged_sizes(own, SEGS, LEN, LEN // 4, 0)), jnp.arange(LEN), side="right"))(jax.random.split(key_of[2], N_DP)).reshape((N_DP, LEN)).astype(jnp.int32),
        "frozen_base_levels": jnp.clip(jax.random.uniform(key_of[3], (MODEL_WIDTH, KEY_FEATURES), jnp.float32, -1.0, 1.0) * block_levels(key_of[3], (MODEL_WIDTH, KEY_FEATURES), ((0, 16),), -0.4, 0.0), -1.0, 1.0).astype(jnp.bfloat16),
        "first_level_scales": jnp.clip(jnp.exp(math.log(2.0) - 1.3862944 * jax.random.uniform(key_of[4], (MODEL_WIDTH // BLOCK, KEY_FEATURES), jnp.float32) ** block_levels(key_of[4], (MODEL_WIDTH // BLOCK, KEY_FEATURES), ((0, 16),), -0.2, 0.2)), 0.5, 2.0).astype(jnp.bfloat16),
        "second_level_scales": jnp.clip(jnp.exp(jax.random.uniform(key_of[5], (MODEL_WIDTH // (BLOCK * SGROUP), KEY_FEATURES), jnp.float32, math.log(0.01), math.log(0.03))), 0.01, 0.03),
        "adapter_down_matrix": bell_draw(key_of[6], (MODEL_WIDTH, ADAPTER_RANK), MODEL_WIDTH ** -0.5, 0.046875, ((0, 16),)),
        "adapter_up_matrix": bell_draw(key_of[7], (ADAPTER_RANK, KEY_FEATURES), ADAPTER_RANK ** -0.5, 0.75),
    }


rope_base = 500000.0

def unrotate(input_gradients, position):
    token_row_list = input_gradients.shape[0]
    shaped = input_gradients.astype(jnp.float32).reshape(token_row_list, -1, HEAD)
    half = HEAD // 2
    freqs = rope_base ** (-jnp.arange(half, dtype=jnp.float32) * 2.0 / HEAD)
    angle = position.astype(jnp.float32)[:, None, None] * freqs[None, None, :]
    cosine = jnp.cos(angle)
    sine = jnp.sin(angle)
    first = shaped[..., :half]
    second = shaped[..., half:]
    out_first = first * cosine + second * sine
    out_second = second * cosine - first * sine
    return jnp.concatenate([out_first, out_second], -1).reshape(token_row_list, -1).astype(jnp.bfloat16)

def positions_of(document_numbers):
    marks = jnp.arange(SEGS, dtype=jnp.int32)
    onehot = (document_numbers[:, :, None] == marks[None, None, :]).astype(jnp.int32)
    counts = lax.optimization_barrier(jnp.sum(onehot, axis=1))
    before = jnp.cumsum(counts, axis=1) - counts
    first = lax.optimization_barrier(jnp.sum(onehot * before[:, None, :], axis=-1))
    return jnp.arange(LEN, dtype=jnp.int32)[None, :] - first

def reference(tokens, rotated_key_gradient, document_numbers, frozen_base_levels, first_level_scales, second_level_scales, adapter_down_matrix, adapter_up_matrix):
    adapter_scale = 16.0 / ADAPTER_RANK
    blocks = MODEL_WIDTH // BLOCK
    scaled = frozen_base_levels.astype(jnp.float32).reshape(blocks, BLOCK, KEY_FEATURES) * first_level_scales.astype(jnp.float32)[:, None, :]
    per_block = jnp.repeat(second_level_scales, SGROUP, axis=0)
    weight = (scaled * per_block[:, None, :]).reshape(MODEL_WIDTH, KEY_FEATURES).astype(jnp.bfloat16)
    position = positions_of(document_numbers)
    seq_tokens = tokens.reshape(N_DP, LEN, MODEL_WIDTH)
    seq_grads = rotated_key_gradient.reshape(N_DP, LEN, KEY_FEATURES)

    def one_sequence(carry, items):
        down_sum, up_sum = carry
        token_row_list, outer, place = items
        input_gradients = unrotate(outer, place)
        reduced_gradient = jnp.dot(input_gradients, adapter_up_matrix.T, preferred_element_type=jnp.float32).astype(jnp.bfloat16)
        frozen_base_term = jnp.dot(input_gradients, weight.T, preferred_element_type=jnp.float32)
        adapter_term = jnp.dot(reduced_gradient, adapter_down_matrix.T, preferred_element_type=jnp.float32)
        gradient_token_rows = (frozen_base_term + adapter_scale * adapter_term).astype(jnp.bfloat16)
        reduced_tokens = jnp.dot(token_row_list, adapter_down_matrix, preferred_element_type=jnp.float32).astype(jnp.bfloat16)
        down_sum = down_sum + jnp.dot(token_row_list.T, reduced_gradient, preferred_element_type=jnp.float32)
        up_sum = up_sum + jnp.dot(reduced_tokens.T, input_gradients, preferred_element_type=jnp.float32)
        return ((down_sum, up_sum), gradient_token_rows)
    start = (jnp.zeros((MODEL_WIDTH, ADAPTER_RANK), jnp.float32), jnp.zeros((ADAPTER_RANK, KEY_FEATURES), jnp.float32))
    (down_sum, up_sum), gradient_token_rows = lax.scan(one_sequence, start, (seq_tokens, seq_grads, position))
    factor = adapter_scale / jnp.sqrt(jnp.float32(TOKENS))
    return (gradient_token_rows.reshape(TOKENS, MODEL_WIDTH), factor * down_sum, factor * up_sum)
```

```python
import functools

import jax
import jax.numpy as jnp
from jax import lax
from jax.experimental import pallas as pl
from jax.experimental.pallas import tpu as pltpu
from jax.sharding import Mesh, PartitionSpec as P

HEAD = 128
RANK = 64
BLOCK = 64
WIDTH = 16384
KEYS = 512
ROWS = 160
SHARDS = 16
NZ = 8
HALF = 512
QUART = 256
ROPE_BASE = 500000.0
SCALE = 16.0 / RANK
TOKENS = 40960

BF = jnp.bfloat16
F32 = jnp.float32

X_AXES = ("xh", "c", "xl")
SHARD_AXES = ("xl", "z")
DP_AXES = ("xh", "y", "c")


def params(mib):
    return pltpu.CompilerParams(vmem_limit_bytes=mib * 1024 * 1024)


def dot(a, b, ca, cb):
    return lax.dot_general(a, b, (((ca,), (cb,)), ((), ())), preferred_element_type=F32)


def weight_kernel(idx, levels, scales, second, down, up, out):
    base = dot(down[...], up[...], 1, 0) * SCALE
    for j in range(HALF // BLOCK):
        rows = slice(j * BLOCK, (j + 1) * BLOCK)
        first = scales[j : j + 1, :].astype(F32)
        scaled = (levels[rows, :].astype(F32) * first) * second[...]
        out[rows, :] = (scaled + base[rows, :]).astype(BF)


def local_weight(idx, levels, scales, second, down, up):
    return pl.pallas_call(
        weight_kernel,
        grid_spec=pltpu.PrefetchScalarGridSpec(
            num_scalar_prefetch=1,
            grid=(1,),
            in_specs=[
                pl.BlockSpec((HALF, KEYS), lambda i, s: (s[0], 0)),
                pl.BlockSpec((HALF // BLOCK, KEYS), lambda i, s: (s[0], 0)),
                pl.BlockSpec((1, KEYS), lambda i, s: (0, 0)),
                pl.BlockSpec((HALF, RANK), lambda i, s: (s[0], 0)),
                pl.BlockSpec((RANK, KEYS), lambda i, s: (0, 0)),
            ],
            out_specs=pl.BlockSpec((HALF, KEYS), lambda i, s: (0, 0)),
        ),
        out_shape=jax.ShapeDtypeStruct((HALF, KEYS), BF),
        compiler_params=params(16),
        cost_estimate=pl.CostEstimate(flops=2 * HALF * RANK * KEYS, bytes_accessed=2 << 20, transcendentals=0),
        name="weight",
    )(idx, levels, scales, second, down, up)


def grads_kernel(idx, everyone, own, rotated, freqs, up, grads, low):
    mine = own[...]
    count = jnp.zeros((ROWS, QUART), F32)
    for k in range(SHARDS):
        row = everyone[k, RANK : RANK + 1, :].astype(F32)
        count = count + jnp.where(row < mine, 1.0, 0.0)
    first = jnp.sum(count, axis=1, keepdims=True)
    place = lax.broadcasted_iota(jnp.int32, (ROWS, 1), 0) + idx[3] * ROWS
    position = place.astype(F32) - first
    angle = position * freqs[...]
    cosine = jnp.cos(angle)
    lane = lax.broadcasted_iota(jnp.int32, (ROWS, HEAD), 1)
    sine = jnp.where(lane < HEAD // 2, 1.0, -1.0) * jnp.sin(angle)
    for h in range(KEYS // HEAD):
        cols = slice(h * HEAD, (h + 1) * HEAD)
        g = rotated[:, cols].astype(F32)
        grads[:, cols] = (g * cosine + pltpu.roll(g, HEAD // 2, 1) * sine).astype(BF)
    low[...] = dot(up[...], grads[...], 1, 1).astype(BF)


def make_grads(idx, everyone, own, rotated, freqs, up):
    full = lambda shape: pl.BlockSpec(shape, lambda i, s: (0,) * len(shape))
    return pl.pallas_call(
        grads_kernel,
        grid_spec=pltpu.PrefetchScalarGridSpec(
            num_scalar_prefetch=1,
            grid=(1,),
            in_specs=[
                full(everyone.shape),
                full((ROWS, 1)),
                full((ROWS, KEYS)),
                full((1, HEAD)),
                full((RANK, KEYS)),
            ],
            out_specs=[full((ROWS, KEYS)), full((RANK, ROWS))],
        ),
        out_shape=[jax.ShapeDtypeStruct((ROWS, KEYS), BF), jax.ShapeDtypeStruct((RANK, ROWS), BF)],
        compiler_params=params(16),
        cost_estimate=pl.CostEstimate(flops=2 * ROWS * RANK * KEYS, bytes_accessed=1 << 20, transcendentals=2 * ROWS * HEAD),
        name="grads",
    )(idx, everyone, own, rotated, freqs, up)


DOWN_STEPS = 4
DOWN_SHARDS = SHARDS // DOWN_STEPS


def down_kernel(idx, low, tokens, keep, send):
    c = idx[0]
    for k in range(DOWN_SHARDS):
        cols = slice(k * HALF, (k + 1) * HALF)
        mine = pl.multiple_of(k * 2 * HALF + c * HALF, HALF)
        other = pl.multiple_of(k * 2 * HALF + (1 - c) * HALF, HALF)
        send[:, cols] = dot(low[...], tokens[:, pl.ds(other, HALF)], 1, 0).astype(BF)
        keep[:, cols] = dot(low[...], tokens[:, pl.ds(mine, HALF)], 1, 0)


def down_part(idx, low, tokens):
    wide = DOWN_SHARDS * HALF
    return pl.pallas_call(
        down_kernel,
        grid_spec=pltpu.PrefetchScalarGridSpec(
            num_scalar_prefetch=1,
            grid=(DOWN_STEPS,),
            in_specs=[
                pl.BlockSpec((RANK, ROWS), lambda i, s: (0, 0)),
                pl.BlockSpec((ROWS, 2 * wide), lambda i, s: (0, i)),
            ],
            out_specs=[
                pl.BlockSpec((RANK, wide), lambda i, s: (0, i)),
                pl.BlockSpec((RANK, wide), lambda i, s: (0, i)),
            ],
        ),
        out_shape=[
            jax.ShapeDtypeStruct((RANK, WIDTH // 2), F32),
            jax.ShapeDtypeStruct((RANK, WIDTH // 2), BF),
        ],
        compiler_params=params(24),
        cost_estimate=pl.CostEstimate(flops=2 * ROWS * RANK * WIDTH, bytes_accessed=9 << 20, transcendentals=0),
        name="down",
    )(idx, low, tokens)


def up_kernel(idx, t0, t1, t2, t3, a0, a1, a2, a3, grads, keep, send, total):
    i = pl.program_id(0)

    @pl.when(i == 0)
    def _():
        total[...] = jnp.zeros_like(total)

    part = dot(t0[...], a0[0], 1, 1) + dot(t1[...], a1[0], 1, 1)
    total[...] += part + (dot(t2[...], a2[0], 1, 1) + dot(t3[...], a3[0], 1, 1))

    @pl.when(i == SHARDS - 1)
    def _():
        low = total[...].astype(BF)
        mine = pl.multiple_of(idx[0] * QUART, QUART)
        other = pl.multiple_of((1 - idx[0]) * QUART, QUART)
        keep[...] = dot(low, grads[:, pl.ds(mine, QUART)], 0, 0)
        send[...] = dot(low, grads[:, pl.ds(other, QUART)], 0, 0)


def up_part(idx, tokens, pieces, grads):
    def column(flip_c, flip_x):
        def at(i, s):
            c = s[0] if not flip_c else 1 - s[0]
            x = s[1] if not flip_x else 1 - s[1]
            return (0, i * 4 + c * 2 + x)

        return pl.BlockSpec((ROWS, QUART), at)

    piece = pl.BlockSpec((1, RANK, QUART), lambda i, s: (i, 0, 0))
    full = lambda shape: pl.BlockSpec(shape, lambda i, s: (0,) * len(shape))
    return pl.pallas_call(
        up_kernel,
        grid_spec=pltpu.PrefetchScalarGridSpec(
            num_scalar_prefetch=1,
            grid=(SHARDS,),
            in_specs=[column(0, 0), column(0, 1), column(1, 0), column(1, 1)]
            + [piece] * 4
            + [full((ROWS, KEYS))],
            out_specs=[full((RANK, QUART)), full((RANK, QUART))],
            scratch_shapes=[pltpu.VMEM((ROWS, RANK), F32)],
        ),
        out_shape=[jax.ShapeDtypeStruct((RANK, QUART), F32)] * 2,
        compiler_params=params(16),
        cost_estimate=pl.CostEstimate(flops=2 * ROWS * RANK * WIDTH, bytes_accessed=8 << 20, transcendentals=0),
        name="up",
    )(idx, tokens, tokens, tokens, tokens, *pieces, grads)


def block_kernel(n_weights, *refs):
    sources = refs[:4]
    weights = refs[4 : 4 + n_weights]
    outs = refs[4 + n_weights :]
    for source, out in zip(sources[::-1], outs[::-1]):
        at = 0
        for w in weights:
            wide = w.shape[0]
            out[:, at : at + wide] = dot(source[...], w[...], 1, 1).astype(BF)
            at += wide


def blocks(sources, weights):
    wide = sum(w.shape[0] for w in weights)
    return pl.pallas_call(
        functools.partial(block_kernel, len(weights)),
        out_shape=[jax.ShapeDtypeStruct((ROWS, wide), BF)] * 4,
        compiler_params=params(24),
        cost_estimate=pl.CostEstimate(
            flops=2 * 4 * ROWS * KEYS * wide, bytes_accessed=2 * wide * (KEYS + 4 * ROWS), transcendentals=0
        ),
        name="blocks",
    )(*sources, *weights)


def assemble_kernel(groups, idx, *refs):
    n = 4 * len(groups)
    pieces, out, sems = refs[:n], refs[n], refs[n + 1]
    c, x, z = idx[0], idx[2], idx[4]
    copies = []
    for g, offsets in enumerate(groups):
        for q in range(4):
            xl = x if q < 2 else 1 - x
            h = c if q % 2 == 0 else 1 - c
            for j, k in enumerate(offsets):
                zz = lax.rem(z + (k + NZ), NZ)
                col = pl.multiple_of(((xl * NZ + zz) * 2 + h) * HALF, HALF)
                copies.append(
                    pltpu.make_async_copy(
                        pieces[4 * g + q].at[:, pl.ds(j * HALF, HALF)],
                        out.at[:, pl.ds(col, HALF)],
                        sems.at[len(copies)],
                    )
                )
    for copy in copies:
        copy.start()
    for copy in copies:
        copy.wait()


def assemble(idx, groups, pieces):
    anywhere = pl.BlockSpec(memory_space=pl.ANY)
    return pl.pallas_call(
        functools.partial(assemble_kernel, groups),
        in_specs=[pl.BlockSpec(memory_space=pltpu.SMEM)] + [anywhere] * len(pieces),
        out_specs=anywhere,
        scratch_shapes=[pltpu.SemaphoreType.DMA((32,))],
        out_shape=jax.ShapeDtypeStruct((ROWS, WIDTH), BF),
        compiler_params=params(8),
        cost_estimate=pl.CostEstimate(flops=0, bytes_accessed=10 << 20, transcendentals=0),
        name="assemble",
    )(idx, *pieces)


def x_permutation(swap):
    at = lambda x, c: ((x // 2) * 2 + c) * 2 + x % 2
    pairs = []
    for x in range(4):
        for c in range(2):
            if (c ^ swap) == 0:
                pairs.append((at(x, c), at((x + 1) % 4, 0)))
            else:
                pairs.append((at(x, c), at((x - 1) % 4, 1)))
    return pairs


def inverse(pairs):
    return [(b, a) for a, b in pairs]


CORE = [(0, 1), (1, 0)]
RIGHT = [(i, (i + 1) % NZ) for i in range(NZ)]
LEFT = [(i, (i - 1) % NZ) for i in range(NZ)]


def on_device(tokens, rotated, documents, levels, scales, second, down, up):
    xh, y, c, xl, z = (lax.axis_index(a) for a in ("xh", "y", "c", "xl", "z"))
    idx = jnp.stack([c, xh, xl, xl * NZ + z, z]).astype(jnp.int32)

    weight = local_weight(idx, levels, scales, second, down, up)
    right = [weight]
    left = [weight]
    for step in range(3):
        right.append(lax.ppermute(right[-1], "z", RIGHT))
        left.append(lax.ppermute(left[-1], "z", LEFT))
    far = HALF // 2
    far_right = lax.ppermute(right[-1][:far], "z", RIGHT)
    far_left = lax.ppermute(left[-1][far:], "z", LEFT)

    quarter = lax.dynamic_slice(down, ((c * 2 + xh) * QUART, 0), (QUART, RANK)).T
    ids = jnp.pad(documents.astype(BF), ((0, 7), (0, QUART - ROWS)), constant_values=1000.0)
    packet = jnp.concatenate([quarter, ids], axis=0)
    packet = jnp.broadcast_to(packet[None], (SHARDS,) + packet.shape)
    everyone = lax.all_to_all(packet, SHARD_AXES, 0, 0, tiled=True)

    half = HEAD // 2
    freqs = ROPE_BASE ** (-jnp.arange(half, dtype=F32) * 2.0 / HEAD)
    freqs = jnp.concatenate([freqs, freqs])[None, :]
    own = documents.astype(F32).reshape(ROWS, 1)
    grads, low = make_grads(idx, everyone, own, rotated, freqs, up)

    there, across = x_permutation(0), x_permutation(1)
    sources = [
        grads,
        lax.ppermute(grads, "c", CORE),
        lax.ppermute(grads, X_AXES, there),
        lax.ppermute(grads, X_AXES, across),
    ]

    keep, send = down_part(idx, low, tokens)
    total = keep + lax.ppermute(send, "c", CORE).astype(F32)
    total = total.reshape(4, RANK // 4, WIDTH // 2)
    mine = lax.dynamic_index_in_dim(total, y, 0, keepdims=False)
    for d in (1, 3, 2):
        out = lax.dynamic_index_in_dim(total, (y + d) % 4, 0, keepdims=False).astype(BF)
        mine = mine + lax.ppermute(out, "y", [(i, (i + d) % 4) for i in range(4)]).astype(F32)

    other_x = lax.ppermute(everyone, "xh", CORE)
    pieces = [everyone, other_x, lax.ppermute(everyone, "c", CORE), lax.ppermute(other_x, "c", CORE)]
    up_keep, up_send = up_part(idx, tokens, pieces, grads)
    up_total = (up_keep + lax.ppermute(up_send, "c", CORE)).reshape(4, RANK // 4, QUART)
    up_mine = lax.dynamic_index_in_dim(up_total, y, 0, keepdims=False)
    for d in (1, 3, 2):
        out = lax.dynamic_index_in_dim(up_total, (y + d) % 4, 0, keepdims=False)
        up_mine = up_mine + lax.ppermute(out, "y", [(i, (i + d) % 4) for i in range(4)])

    slabs = mine.reshape(RANK // 4, SHARDS, HALF).transpose(1, 0, 2)
    slabs = jnp.concatenate([slabs, jnp.broadcast_to(up_mine[None], (SHARDS,) + up_mine.shape)], axis=2)
    slabs = jnp.sum(lax.all_to_all(slabs, SHARD_AXES, 0, 0, tiled=True), axis=0)
    slabs = jnp.broadcast_to(slabs[None], (16,) + slabs.shape)
    slabs = lax.all_to_all(slabs, DP_AXES, 0, 0, tiled=True)
    slabs = slabs.reshape(2, 4, 2, RANK // 4, HALF + QUART)
    factor = SCALE / jnp.sqrt(jnp.float32(TOKENS))
    slabs = factor * (slabs[0] + slabs[1])
    grad_down = slabs[..., :HALF].transpose(1, 3, 0, 2).reshape(2 * HALF, RANK)
    grad_up = slabs[..., HALF:].transpose(0, 2, 1, 3).reshape(RANK, KEYS)

    groups = ((0, -1, 1), (-2, 2, -3, 3), (4,))
    parts = (
        (right[0], right[1], left[1]),
        (right[2], left[2], right[3], left[3]),
        (far_right, far_left),
    )
    filled = []
    for part in parts:
        o, p, a, b = blocks(sources, part)
        filled += [
            o,
            lax.ppermute(p, "c", CORE),
            lax.ppermute(a, X_AXES, inverse(there)),
            lax.ppermute(b, X_AXES, inverse(across)),
        ]
    grad_tokens = assemble(idx, groups, filled)
    return grad_tokens, grad_down, grad_up


def solution(mesh):
    fine = Mesh(mesh.devices.reshape(2, 4, 2, 2, 8), ("xh", "y", "c", "xl", "z"))
    everything = DP_AXES + SHARD_AXES
    in_specs = (
        P(everything, None),
        P(everything, None),
        P(DP_AXES, SHARD_AXES),
        P(SHARD_AXES, None),
        P(SHARD_AXES, None),
        P(),
        P(SHARD_AXES, None),
        P(),
    )
    out_specs = (P(everything, None), P(SHARD_AXES, None), P())
    return jax.shard_map(on_device, mesh=fine, in_specs=in_specs, out_specs=out_specs, check_vma=False)
```

```python
import functools

import jax
import jax.numpy as jnp
from jax import lax
from jax.experimental import pallas as pl
from jax.experimental.pallas import tpu as pltpu
from jax.sharding import Mesh, PartitionSpec as P

HEAD = 128
RANK = 64
BLOCK = 64
WIDTH = 16384
KEYS = 512
ROWS = 160
SHARDS = 16
NZ = 8
HALF = 512
PACKET = NZ * RANK + ROWS
IDS = 16
ROPE_BASE = 500000.0
SCALE = 16.0 / RANK
TOKENS = 40960

BF = jnp.bfloat16
F32 = jnp.float32

X_AXES = ("xh", "c", "xl")
SHARD_AXES = ("xl", "z")
DP_AXES = ("xh", "y", "c")


BRIEF = pl.CostEstimate(flops=1, bytes_accessed=1, transcendentals=0)


def params(mib):
    return pltpu.CompilerParams(vmem_limit_bytes=mib * 1024 * 1024)


def dot(a, b, ca, cb):
    return lax.dot_general(a, b, (((ca,), (cb,)), ((), ())), preferred_element_type=F32)


def weight_kernel(idx, levels, scales, second, down, up, ids, weight, packet):
    half = down[...]
    for k in range(NZ):
        packet[k, :RANK, :] = half
        packet[k, RANK:, :] = ids[...]
    scale = scales[...].astype(F32)
    n = HALF // BLOCK
    scale = jnp.where(idx[0] == 0, scale[:n], scale[n:])
    rows = []
    for j in range(n):
        level = levels[j * BLOCK : (j + 1) * BLOCK, :].astype(F32)
        rows.append((level * scale[j : j + 1]) * second[...])
    base = dot(up[...], half, 0, 0) * SCALE
    weight[...] = (jnp.concatenate(rows, axis=0).T + base).astype(BF)


def local_weight(idx, levels, scales, second, down, up, ids):
    full = lambda shape: pl.BlockSpec(shape, lambda i, s: (0,) * len(shape))
    return pl.pallas_call(
        weight_kernel,
        grid_spec=pltpu.PrefetchScalarGridSpec(
            num_scalar_prefetch=1,
            grid=(1,),
            in_specs=[
                pl.BlockSpec((HALF, KEYS), lambda i, s: (s[0], 0)),
                full(scales.shape),
                full((1, KEYS)),
                pl.BlockSpec((RANK, HALF), lambda i, s: (0, s[0])),
                full((RANK, KEYS)),
                full((IDS, HALF)),
            ],
            out_specs=[full((KEYS, HALF)), full((NZ, RANK + IDS, HALF))],
        ),
        out_shape=[
            jax.ShapeDtypeStruct((KEYS, HALF), BF),
            jax.ShapeDtypeStruct((NZ, RANK + IDS, HALF), BF),
        ],
        compiler_params=params(56),
        cost_estimate=BRIEF,
        name="weight",
    )(idx, levels, scales, second, down, up, ids)


def grads_kernel(idx, everyone, own, rotated, freqs, up, packet, low):
    mine = own[...]
    count = jnp.zeros((ROWS, HALF), F32)
    for k in range(NZ):
        packet[k * RANK : (k + 1) * RANK, :] = everyone[k, :RANK, :]
        row = everyone[k, RANK : RANK + 1, :].astype(F32)
        count = count + jnp.where(row < mine, 1.0, 0.0)
    first = jnp.sum(count, axis=1, keepdims=True)
    place = lax.broadcasted_iota(jnp.int32, (ROWS, 1), 0) + idx[3] * ROWS
    position = place.astype(F32) - first
    angle = position * freqs[...]
    cosine = jnp.cos(angle)
    lane = lax.broadcasted_iota(jnp.int32, (ROWS, HEAD), 1)
    sine = jnp.where(lane < HEAD // 2, 1.0, -1.0) * jnp.sin(angle)
    for h in range(KEYS // HEAD):
        cols = slice(h * HEAD, (h + 1) * HEAD)
        g = rotated[:, cols].astype(F32)
        packet[NZ * RANK :, cols] = (g * cosine + pltpu.roll(g, HEAD // 2, 1) * sine).astype(BF)
    low[...] = dot(up[...], packet[NZ * RANK :, :], 1, 1).astype(BF)


def make_grads(idx, everyone, own, rotated, freqs, up):
    full = lambda shape: pl.BlockSpec(shape, lambda i, s: (0,) * len(shape))
    return pl.pallas_call(
        grads_kernel,
        grid_spec=pltpu.PrefetchScalarGridSpec(
            num_scalar_prefetch=1,
            grid=(1,),
            in_specs=[
                full(everyone.shape),
                full((ROWS, 1)),
                full((ROWS, KEYS)),
                full((1, HEAD)),
                full((RANK, KEYS)),
            ],
            out_specs=[full((PACKET, KEYS)), full((RANK, ROWS))],
        ),
        out_shape=[jax.ShapeDtypeStruct((PACKET, KEYS), BF), jax.ShapeDtypeStruct((RANK, ROWS), BF)],
        compiler_params=params(56),
        cost_estimate=BRIEF,
        name="grads",
    )(idx, everyone, own, rotated, freqs, up)


CHUNKS = 8
WIDE = WIDTH // CHUNKS
STEP = WIDE // (2 * HALF)


def down_kernel(idx, low, tokens, keep, send, held, keep_held, send_held, sems):
    c = idx[0]
    loads = [
        pltpu.make_async_copy(tokens.at[:, pl.ds(i * WIDE, WIDE)], held.at[i], sems.at[i]) for i in range(CHUNKS)
    ]
    for load in loads:
        load.start()
    stores = []
    for i in range(CHUNKS):
        loads[i].wait()
        for k in range(STEP):
            at = (i * STEP + k) * HALF
            mine = pl.multiple_of(k * 2 * HALF + c * HALF, HALF)
            other = pl.multiple_of(k * 2 * HALF + (1 - c) * HALF, HALF)
            send_held[:, at : at + HALF] = dot(low[...], held[i, :, pl.ds(other, HALF)], 1, 0).astype(BF)
            keep_held[:, at : at + HALF] = dot(low[...], held[i, :, pl.ds(mine, HALF)], 1, 0)
        cols = pl.ds(i * STEP * HALF, STEP * HALF)
        stores.append(pltpu.make_async_copy(send_held.at[:, cols], send.at[:, cols], sems.at[CHUNKS + 2 * i]))
        stores.append(pltpu.make_async_copy(keep_held.at[:, cols], keep.at[:, cols], sems.at[CHUNKS + 2 * i + 1]))
        stores[-2].start()
        stores[-1].start()
    for store in stores:
        store.wait()


def down_part(idx, low, tokens):
    anywhere = pl.BlockSpec(memory_space=pl.ANY)
    return pl.pallas_call(
        down_kernel,
        in_specs=[pl.BlockSpec(memory_space=pltpu.SMEM), pl.BlockSpec(memory_space=pltpu.VMEM), anywhere],
        out_specs=[anywhere, anywhere],
        out_shape=[
            jax.ShapeDtypeStruct((RANK, WIDTH // 2), F32),
            jax.ShapeDtypeStruct((RANK, WIDTH // 2), BF),
        ],
        scratch_shapes=[
            pltpu.VMEM((CHUNKS, ROWS, WIDE), BF),
            pltpu.VMEM((RANK, WIDTH // 2), F32),
            pltpu.VMEM((RANK, WIDTH // 2), BF),
            pltpu.SemaphoreType.DMA((3 * CHUNKS,)),
        ],
        compiler_params=params(56),
        cost_estimate=BRIEF,
        name="down",
    )(idx, low, tokens)


def up_kernel(idx, tokens, p0, p1, p2, p3, out, held, lows, grads, sems):
    c, x = idx[0], idx[2]
    loads = []
    for i in range(CHUNKS):
        xl = x if i < CHUNKS // 2 else 1 - x
        at = pl.multiple_of(xl * (WIDTH // 2) + (i % (CHUNKS // 2)) * WIDE, WIDE)
        loads.append(pltpu.make_async_copy(tokens.at[:, pl.ds(at, WIDE)], held.at[i], sems.at[i]))
    pieces = [
        pltpu.make_async_copy(p.at[pl.ds(0, NZ * RANK), :], lows.at[k], sems.at[CHUNKS + k])
        for k, p in enumerate((p0, p1, p2, p3))
    ]
    last = pltpu.make_async_copy(p0.at[pl.ds(NZ * RANK, ROWS), :], grads, sems.at[CHUNKS + 4])
    for copy in pieces[:2] + loads[: CHUNKS // 2] + pieces[2:] + loads[CHUNKS // 2 :] + [last]:
        copy.start()
    total = jnp.zeros((ROWS, RANK), F32)
    for i in range(CHUNKS):
        first = 0 if i < CHUNKS // 2 else 2
        if i % (CHUNKS // 2) == 0:
            pieces[first].wait()
            pieces[first + 1].wait()
        loads[i].wait()
        for k in range(STEP):
            z = (i % (CHUNKS // 2)) * STEP + k
            rows = slice(z * RANK, (z + 1) * RANK)
            mine = pl.multiple_of(k * 2 * HALF + c * HALF, HALF)
            other = pl.multiple_of(k * 2 * HALF + (1 - c) * HALF, HALF)
            total = total + dot(held[i, :, pl.ds(mine, HALF)], lows[first, rows, :], 1, 1)
            total = total + dot(held[i, :, pl.ds(other, HALF)], lows[first + 1, rows, :], 1, 1)
    last.wait()
    out[...] = dot(total.astype(BF), grads[...], 0, 0)


def up_part(idx, tokens, packets):
    anywhere = pl.BlockSpec(memory_space=pl.ANY)
    return pl.pallas_call(
        up_kernel,
        in_specs=[pl.BlockSpec(memory_space=pltpu.SMEM)] + [anywhere] * 5,
        out_specs=pl.BlockSpec(memory_space=pltpu.VMEM),
        out_shape=jax.ShapeDtypeStruct((RANK, KEYS), F32),
        scratch_shapes=[
            pltpu.VMEM((CHUNKS, ROWS, WIDE), BF),
            pltpu.VMEM((4, NZ * RANK, HALF), BF),
            pltpu.VMEM((ROWS, KEYS), BF),
            pltpu.SemaphoreType.DMA((CHUNKS + 5,)),
        ],
        compiler_params=params(56),
        cost_estimate=BRIEF,
        name="up",
    )(idx, tokens, *packets)


def block_kernel(own, core, there, across, weight, out_own, out_core, out_there, out_across, rows):
    @pl.when(pl.program_id(0) == 0)
    def _():
        for k, source in enumerate((own, core, there, across)):
            rows[k * ROWS : (k + 1) * ROWS, :] = source[NZ * RANK :, :]

    product = dot(rows[...], weight[...], 1, 0).astype(BF)
    for k, out in enumerate((out_own, out_core, out_there, out_across)):
        out[...] = product[k * ROWS : (k + 1) * ROWS]


def blocks(sources, weight, start, count):
    source = pl.BlockSpec((PACKET, KEYS), lambda i: (0, 0))
    out = pl.BlockSpec((ROWS, HALF), lambda i: (0, i))
    return pl.pallas_call(
        block_kernel,
        grid=(count,),
        in_specs=[source] * 4 + [pl.BlockSpec((KEYS, HALF), lambda i: (start + i, 0))],
        out_specs=[out] * 4,
        out_shape=[jax.ShapeDtypeStruct((ROWS, count * HALF), BF)] * 4,
        scratch_shapes=[pltpu.VMEM((4 * ROWS, KEYS), BF)],
        compiler_params=params(56),
        cost_estimate=BRIEF,
        name="blocks",
    )(*sources, weight)


def assemble_kernel(start, count, idx, own, core, there, across, *rest):
    out, sems = rest[-2:]
    copies = []
    for k, piece in enumerate((own, core, there, across)):
        x = idx[2] if k < 2 else 1 - idx[2]
        h = idx[0] if k % 2 == 0 else 1 - idx[0]
        for j in range(count):
            col = pl.multiple_of(((x * NZ + start + j) * 2 + h) * HALF, HALF)
            copies.append(
                pltpu.make_async_copy(
                    piece.at[:, pl.ds(j * HALF, HALF)],
                    out.at[:, pl.ds(col, HALF)],
                    sems.at[len(copies)],
                )
            )
    for copy in copies:
        copy.start()
    for copy in copies:
        copy.wait()


def assemble(idx, pieces, start, count, before):
    anywhere = pl.BlockSpec(memory_space=pl.ANY)
    return pl.pallas_call(
        functools.partial(assemble_kernel, start, count),
        in_specs=[pl.BlockSpec(memory_space=pltpu.SMEM)]
        + [pl.BlockSpec(memory_space=pltpu.VMEM)] * 4
        + [anywhere] * len(before),
        out_specs=anywhere,
        scratch_shapes=[pltpu.SemaphoreType.DMA((4 * count,))],
        out_shape=jax.ShapeDtypeStruct((ROWS, WIDTH), BF),
        input_output_aliases={5: 0} if before else {},
        compiler_params=params(8),
        cost_estimate=BRIEF,
        name="assemble",
    )(idx, *pieces, *before)


def x_permutation(swap):
    at = lambda x, c: ((x // 2) * 2 + c) * 2 + x % 2
    pairs = []
    for x in range(4):
        for c in range(2):
            if (c ^ swap) == 0:
                pairs.append((at(x, c), at((x + 1) % 4, 0)))
            else:
                pairs.append((at(x, c), at((x - 1) % 4, 1)))
    return pairs


def inverse(pairs):
    return [(b, a) for a, b in pairs]


CORE = [(0, 1), (1, 0)]


def on_device(tokens, rotated, documents, levels, scales, second, down, up):
    xh, y, c, xl, z = (lax.axis_index(a) for a in ("xh", "y", "c", "xl", "z"))
    idx = jnp.stack([c, xh, xl, xl * NZ + z]).astype(jnp.int32)

    ids = jnp.pad(documents.astype(BF), ((0, 0), (0, HALF // 2 - ROWS)), constant_values=1000.0)
    ids = jnp.concatenate([ids, lax.ppermute(ids, "xl", CORE)], axis=1)
    ids = jnp.broadcast_to(ids, (IDS, HALF))

    weight, packet = local_weight(idx, levels, scales, second, down.T, up, ids)
    weight = lax.all_gather(weight, "z", tiled=True)
    everyone = lax.all_to_all(packet, "z", 0, 0, tiled=True)

    half = HEAD // 2
    freqs = ROPE_BASE ** (-jnp.arange(half, dtype=F32) * 2.0 / HEAD)
    freqs = jnp.concatenate([freqs, freqs])[None, :]
    own = documents.astype(F32).reshape(ROWS, 1)
    packet, low = make_grads(idx, everyone, own, rotated, freqs, up)

    there, across = x_permutation(0), x_permutation(1)
    packets = [
        packet,
        lax.ppermute(packet, "c", CORE),
        lax.ppermute(packet, X_AXES, there),
        lax.ppermute(packet, X_AXES, across),
    ]

    keep, send = down_part(idx, low, tokens)
    sent = [lax.ppermute(part, "c", CORE) for part in jnp.split(send, 2, axis=0)]
    total = keep + jnp.concatenate(sent, axis=0).astype(F32)
    total = total.reshape(4, RANK // 4, WIDTH // 2)
    mine = lax.dynamic_index_in_dim(total, y, 0, keepdims=False)
    for d in (1, 3, 2):
        out = lax.dynamic_index_in_dim(total, (y + d) % 4, 0, keepdims=False).astype(BF)
        mine = mine + lax.ppermute(out, "y", [(i, (i + d) % 4) for i in range(4)]).astype(F32)

    up_total = up_part(idx, tokens, packets).reshape(8, 8, KEYS)
    up_total = jnp.sum(lax.all_to_all(up_total, ("y", "c"), 0, 0, tiled=True), axis=0)

    slabs = mine.reshape(RANK // 4, SHARDS, HALF).transpose(1, 0, 2)
    up_total = jnp.broadcast_to(up_total[None], (SHARDS,) + up_total.shape)
    slabs = jnp.concatenate([slabs, up_total], axis=1).astype(BF)
    slabs = lax.all_to_all(slabs, SHARD_AXES, 0, 0, tiled=True)
    slabs = jnp.sum(slabs.astype(F32), axis=0).astype(BF)
    slabs = jnp.broadcast_to(slabs[None], (16,) + slabs.shape)
    slabs = lax.all_to_all(slabs, DP_AXES, 0, 0, tiled=True).astype(F32)
    slabs = slabs.reshape(2, 4, 2, RANK // 4 + 8, KEYS)
    factor = SCALE / jnp.sqrt(jnp.float32(TOKENS))
    slabs = factor * (slabs[0] + slabs[1])
    grad_down = slabs[:, :, : RANK // 4].transpose(1, 3, 0, 2).reshape(2 * HALF, RANK)
    grad_up = slabs[:, :, RANK // 4 :].reshape(RANK, KEYS)

    grad_tokens = []
    for start, count in ((0, 4), (4, 4)):
        o, p, a, b = blocks(packets, weight, start, count)
        pieces = [
            o,
            lax.ppermute(p, "c", CORE),
            lax.ppermute(a, X_AXES, inverse(there)),
            lax.ppermute(b, X_AXES, inverse(across)),
        ]
        grad_tokens = [assemble(idx, pieces, start, count, grad_tokens)]
    grad_tokens = grad_tokens[0]
    return grad_tokens, grad_down, grad_up


def solution(mesh):
    fine = Mesh(mesh.devices.reshape(2, 4, 2, 2, 8), ("xh", "y", "c", "xl", "z"))
    everything = DP_AXES + SHARD_AXES
    in_specs = (
        P(everything, None),
        P(everything, None),
        P(DP_AXES, SHARD_AXES),
        P(SHARD_AXES, None),
        P(SHARD_AXES, None),
        P(),
        P(SHARD_AXES, None),
        P(),
    )
    out_specs = (P(everything, None), P(SHARD_AXES, None), P())
    return jax.shard_map(on_device, mesh=fine, in_specs=in_specs, out_specs=out_specs, check_vma=False)
```

```python
import functools

import jax
import jax.numpy as jnp
from jax import lax
from jax.experimental import pallas as pl
from jax.experimental.pallas import tpu as pltpu
from jax.sharding import Mesh, PartitionSpec as P

HEAD = 128
RANK = 64
BLOCK = 64
WIDTH = 16384
KEYS = 512
ROWS = 160
SHARDS = 16
NZ = 8
HALF = 512
LANES = 128
IDS = 16
ROPE_BASE = 500000.0
SCALE = 16.0 / RANK
TOKENS = 40960

BF = jnp.bfloat16
F32 = jnp.float32

X_AXES = ("xh", "c", "xl")
SHARD_AXES = ("xl", "z")
DP_AXES = ("xh", "y", "c")


BRIEF = pl.CostEstimate(flops=1, bytes_accessed=1, transcendentals=0)


def params(mib):
    return pltpu.CompilerParams(vmem_limit_bytes=mib * 1024 * 1024)


def dot(a, b, ca, cb):
    return lax.dot_general(a, b, (((ca,), (cb,)), ((), ())), preferred_element_type=F32)


def weight_kernel(idx, levels, scales, second, down, up, weight):
    scale = scales[...].astype(F32)
    n = HALF // BLOCK
    scale = jnp.where(idx[0] == 0, scale[:n], scale[n:])
    rows = []
    for j in range(n):
        level = levels[j * BLOCK : (j + 1) * BLOCK, :].astype(F32)
        rows.append((level * scale[j : j + 1]) * second[...])
    base = dot(up[...], down[...], 0, 0) * SCALE
    weight[...] = (jnp.concatenate(rows, axis=0).T + base).astype(BF)


def local_weight(idx, levels, scales, second, down, up):
    full = lambda shape: pl.BlockSpec(shape, lambda i, s: (0,) * len(shape))
    return pl.pallas_call(
        weight_kernel,
        grid_spec=pltpu.PrefetchScalarGridSpec(
            num_scalar_prefetch=1,
            grid=(1,),
            in_specs=[
                pl.BlockSpec((HALF, KEYS), lambda i, s: (s[0], 0)),
                full(scales.shape),
                full((1, KEYS)),
                pl.BlockSpec((RANK, HALF), lambda i, s: (0, s[0])),
                full((RANK, KEYS)),
            ],
            out_specs=full((KEYS, HALF)),
        ),
        out_shape=jax.ShapeDtypeStruct((KEYS, HALF), BF),
        compiler_params=params(56),
        cost_estimate=BRIEF,
        name="weight",
    )(idx, levels, scales, second, down, up)


def packet_kernel(idx, down, ids, after, packet):
    for k in range(SHARDS):
        packet[k, :RANK, :] = down[...]
        packet[k, RANK:, :] = ids[...]


def make_packet(idx, down, ids, after):
    full = lambda shape: pl.BlockSpec(shape, lambda i, s: (0,) * len(shape))
    return pl.pallas_call(
        packet_kernel,
        grid_spec=pltpu.PrefetchScalarGridSpec(
            num_scalar_prefetch=1,
            grid=(1,),
            in_specs=[
                pl.BlockSpec((RANK, LANES), lambda i, s: (0, s[0] * 4 + s[4])),
                full((IDS, LANES)),
                pl.BlockSpec(memory_space=pl.ANY),
            ],
            out_specs=full((SHARDS, RANK + IDS, LANES)),
        ),
        out_shape=jax.ShapeDtypeStruct((SHARDS, RANK + IDS, LANES), BF),
        compiler_params=params(56),
        cost_estimate=BRIEF,
        name="packet",
    )(idx, down, ids, after)


def grads_kernel(idx, everyone, own, rotated, freqs, up, grads, low):
    mine = own[...]
    count = jnp.zeros((ROWS, LANES), F32)
    for k in range(SHARDS):
        for r in range(2):
            row = everyone[k, r : r + 1, :].astype(F32)
            count = count + jnp.where(row < mine, 1.0, 0.0)
    first = jnp.sum(count, axis=1, keepdims=True)
    place = lax.broadcasted_iota(jnp.int32, (ROWS, 1), 0) + idx[3] * ROWS
    position = place.astype(F32) - first
    angle = position * freqs[...]
    cosine = jnp.cos(angle)
    lane = lax.broadcasted_iota(jnp.int32, (ROWS, HEAD), 1)
    sine = jnp.where(lane < HEAD // 2, 1.0, -1.0) * jnp.sin(angle)
    for h in range(KEYS // HEAD):
        cols = slice(h * HEAD, (h + 1) * HEAD)
        g = rotated[:, cols].astype(F32)
        grads[:, cols] = (g * cosine + pltpu.roll(g, HEAD // 2, 1) * sine).astype(BF)
    low[...] = dot(up[...], grads[...], 1, 1).astype(BF)


def make_grads(idx, everyone, own, rotated, freqs, up):
    full = lambda shape: pl.BlockSpec(shape, lambda i, s: (0,) * len(shape))
    return pl.pallas_call(
        grads_kernel,
        grid_spec=pltpu.PrefetchScalarGridSpec(
            num_scalar_prefetch=1,
            grid=(1,),
            in_specs=[
                pl.BlockSpec((SHARDS, IDS, LANES), lambda i, s: (0, RANK // IDS, 0)),
                full((ROWS, 1)),
                full((ROWS, KEYS)),
                full((1, HEAD)),
                full((RANK, KEYS)),
            ],
            out_specs=[full((ROWS, KEYS)), full((RANK, ROWS))],
        ),
        out_shape=[jax.ShapeDtypeStruct((ROWS, KEYS), BF), jax.ShapeDtypeStruct((RANK, ROWS), BF)],
        compiler_params=params(56),
        cost_estimate=BRIEF,
        name="grads",
    )(idx, everyone, own, rotated, freqs, up)


CHUNKS = 8
WIDE = WIDTH // CHUNKS
STEP = WIDE // (2 * HALF)


def down_kernel(idx, low, tokens, *refs):
    keep, send, (held, keep_held, send_held, sems) = refs[:4], refs[4:8], refs[8:]
    c, y = idx[0], idx[4]
    loads = [
        pltpu.make_async_copy(tokens.at[:, pl.ds(i * WIDE, WIDE)], held.at[i], sems.at[i]) for i in range(CHUNKS)
    ]
    for load in loads:
        load.start()
    stores = []
    for i in range(CHUNKS):
        loads[i].wait()
        for k in range(STEP):
            at = (i * STEP + k) * HALF
            mine = pl.multiple_of(k * 2 * HALF + c * HALF, HALF)
            other = pl.multiple_of(k * 2 * HALF + (1 - c) * HALF, HALF)
            send_held[:, at : at + HALF] = dot(low[...], held[i, :, pl.ds(other, HALF)], 1, 0).astype(BF)
            keep_held[:, at : at + HALF] = dot(low[...], held[i, :, pl.ds(mine, HALF)], 1, 0)
        if i % 4 == 3:
            cols = pl.ds((i - 3) * STEP * HALF, 4 * STEP * HALF)
            for d in range(4):
                rows = pl.ds(pl.multiple_of(lax.rem(y + d, 4) * 16, 16), 16)
                for source, target in ((send_held, send[d]), (keep_held, keep[d])):
                    sem = sems.at[CHUNKS + len(stores)]
                    stores.append(pltpu.make_async_copy(source.at[rows, cols], target.at[:, cols], sem))
                    stores[-1].start()
    for store in stores:
        store.wait()


def down_part(idx, low, tokens):
    anywhere = pl.BlockSpec(memory_space=pl.ANY)
    return pl.pallas_call(
        down_kernel,
        in_specs=[pl.BlockSpec(memory_space=pltpu.SMEM), pl.BlockSpec(memory_space=pltpu.VMEM), anywhere],
        out_specs=[anywhere] * 8,
        out_shape=[jax.ShapeDtypeStruct((RANK // 4, WIDTH // 2), dtype) for dtype in [F32] * 4 + [BF] * 4],
        scratch_shapes=[
            pltpu.VMEM((CHUNKS, ROWS, WIDE), BF),
            pltpu.VMEM((RANK, WIDTH // 2), F32),
            pltpu.VMEM((RANK, WIDTH // 2), BF),
            pltpu.SemaphoreType.DMA((CHUNKS + 16,)),
        ],
        compiler_params=params(56),
        cost_estimate=BRIEF,
        name="down",
    )(idx, low, tokens)


def up_kernel(idx, tokens, *refs):
    given, (grads, _, out, held, lows, sems) = refs[:2], refs[2:]
    c = idx[0]
    loads = [
        pltpu.make_async_copy(tokens.at[:, pl.ds(i * WIDE, WIDE)], held.at[i], sems.at[i]) for i in range(CHUNKS)
    ]
    pieces = [pltpu.make_async_copy(p, lows.at[k], sems.at[CHUNKS + k]) for k, p in enumerate(given)]
    for copy in pieces + loads:
        copy.start()
    for copy in pieces:
        copy.wait()
    total = jnp.zeros((ROWS, RANK), F32)
    for i in range(CHUNKS):
        loads[i].wait()
        for k in range(STEP):
            for p in range(2):
                h = c if p == 0 else 1 - c
                at = pl.multiple_of(k * 2 * HALF + h * HALF, HALF)
                rows = jnp.concatenate([lows[p, q, i * STEP + k] for q in range(4)], axis=1)
                total = total + dot(held[i, :, pl.ds(at, HALF)], rows, 1, 1)
    out[...] = dot(total.astype(BF), grads[...], 0, 0)


def up_part(idx, tokens, lows, grads, after):
    anywhere = pl.BlockSpec(memory_space=pl.ANY)
    return pl.pallas_call(
        up_kernel,
        in_specs=[pl.BlockSpec(memory_space=pltpu.SMEM)]
        + [anywhere] * 3
        + [pl.BlockSpec(memory_space=pltpu.VMEM)]
        + [anywhere],
        out_specs=pl.BlockSpec(memory_space=pltpu.VMEM),
        out_shape=jax.ShapeDtypeStruct((RANK, KEYS), F32),
        scratch_shapes=[
            pltpu.VMEM((CHUNKS, ROWS, WIDE), BF),
            pltpu.VMEM((2, 4, SHARDS, RANK, LANES), BF),
            pltpu.SemaphoreType.DMA((CHUNKS + 2,)),
        ],
        compiler_params=params(56),
        cost_estimate=BRIEF,
        name="up",
    )(idx, tokens, *lows, grads, after)


def block_kernel(own, core, there, across, weight, o0, o1, o2, o3, rows, held, made, sems):
    loads = [
        pltpu.make_async_copy(weight.at[pl.ds(i * KEYS, KEYS), :], held.at[i], sems.at[4 * NZ + i]) for i in range(NZ)
    ]
    for load in loads:
        load.start()
    for k, source in enumerate((own, core, there, across)):
        rows[k * ROWS : (k + 1) * ROWS, :] = source[...]
    stores = []
    for i in range(NZ):
        loads[i].wait()
        made[i] = dot(rows[...], held[i], 1, 0).astype(BF)
        for k, out in enumerate((o0, o1, o2, o3)):
            stores.append(
                pltpu.make_async_copy(
                    made.at[i, pl.ds(k * ROWS, ROWS), :],
                    out.at[:, pl.ds(i * HALF, HALF)],
                    sems.at[4 * i + k],
                )
            )
            stores[-1].start()
    for store in stores:
        store.wait()


def blocks(sources, weight):
    anywhere = pl.BlockSpec(memory_space=pl.ANY)
    return pl.pallas_call(
        block_kernel,
        in_specs=[pl.BlockSpec(memory_space=pltpu.VMEM)] * 4 + [anywhere],
        out_specs=[anywhere] * 4,
        out_shape=[jax.ShapeDtypeStruct((ROWS, NZ * HALF), BF)] * 4,
        scratch_shapes=[
            pltpu.VMEM((4 * ROWS, KEYS), BF),
            pltpu.VMEM((NZ, KEYS, HALF), BF),
            pltpu.VMEM((NZ, 4 * ROWS, HALF), BF),
            pltpu.SemaphoreType.DMA((5 * NZ,)),
        ],
        compiler_params=params(56),
        cost_estimate=BRIEF,
        name="blocks",
    )(*sources, weight)


def assemble_kernel(start, count, idx, own, core, there, across, *rest):
    out, sems = rest[-2:]
    copies = []
    for k, piece in enumerate((own, core, there, across)):
        x = idx[2] if k < 2 else 1 - idx[2]
        h = idx[0] if k % 2 == 0 else 1 - idx[0]
        for j in range(count):
            col = pl.multiple_of(((x * NZ + start + j) * 2 + h) * HALF, HALF)
            copies.append(
                pltpu.make_async_copy(
                    piece.at[:, pl.ds(j * HALF, HALF)],
                    out.at[:, pl.ds(col, HALF)],
                    sems.at[len(copies)],
                )
            )
    for copy in copies:
        copy.start()
    for copy in copies:
        copy.wait()


def assemble(idx, pieces, start, count, before):
    anywhere = pl.BlockSpec(memory_space=pl.ANY)
    return pl.pallas_call(
        functools.partial(assemble_kernel, start, count),
        in_specs=[pl.BlockSpec(memory_space=pltpu.SMEM)]
        + [pl.BlockSpec(memory_space=pltpu.VMEM)] * 4
        + [anywhere] * len(before),
        out_specs=anywhere,
        scratch_shapes=[pltpu.SemaphoreType.DMA((4 * count,))],
        out_shape=jax.ShapeDtypeStruct((ROWS, WIDTH), BF),
        input_output_aliases={5: 0} if before else {},
        compiler_params=params(8),
        cost_estimate=BRIEF,
        name="assemble",
    )(idx, *pieces, *before)


def x_permutation(swap):
    at = lambda x, c: ((x // 2) * 2 + c) * 2 + x % 2
    pairs = []
    for x in range(4):
        for c in range(2):
            if (c ^ swap) == 0:
                pairs.append((at(x, c), at((x + 1) % 4, 0)))
            else:
                pairs.append((at(x, c), at((x - 1) % 4, 1)))
    return pairs


def inverse(pairs):
    return [(b, a) for a, b in pairs]


CORE = [(0, 1), (1, 0)]


def on_device(tokens, rotated, documents, levels, scales, second, down, up):
    xh, y, c, xl, z = (lax.axis_index(a) for a in ("xh", "y", "c", "xl", "z"))
    idx = jnp.stack([c, xh, xl, xl * NZ + z, y]).astype(jnp.int32)

    weight = local_weight(idx, levels, scales, second, down.T, up)

    ids = jnp.pad(documents.astype(BF), ((0, 0), (0, 2 * LANES - ROWS)), constant_values=1000.0)
    ids = jnp.pad(ids.reshape(2, LANES), ((0, IDS - 2), (0, 0)))
    packet = make_packet(idx, down.T, ids, weight)
    weight = lax.all_gather(weight, "z", tiled=True)
    everyone = lax.all_to_all(packet, SHARD_AXES, 0, 0, tiled=True)

    half = HEAD // 2
    freqs = ROPE_BASE ** (-jnp.arange(half, dtype=F32) * 2.0 / HEAD)
    freqs = jnp.concatenate([freqs, freqs])[None, :]
    own = documents.astype(F32).reshape(ROWS, 1)
    grads, low = make_grads(idx, everyone, own, rotated, freqs, up)

    there, across = x_permutation(0), x_permutation(1)
    sources = [
        grads,
        lax.ppermute(grads, "c", CORE),
        lax.ppermute(grads, X_AXES, there),
        lax.ppermute(grads, X_AXES, across),
    ]

    made = down_part(idx, low, tokens)
    keep, send = made[:4], made[4:]
    sent = [lax.ppermute(part, "c", CORE) for part in send]

    lows = jnp.broadcast_to(everyone[None, :, :RANK], (4, SHARDS, RANK, LANES))
    lows = lax.all_to_all(lows, "y", 0, 0, tiled=True)
    lows, sent = lax.optimization_barrier((lows, sent))
    lows = [lows, lax.ppermute(lows, "c", CORE)]

    total = [a + b.astype(F32) for a, b in zip(keep, sent)]
    mine = total[0]
    for d in (1, 3, 2):
        mine = mine + lax.ppermute(total[d].astype(BF), "y", [(i, (i + d) % 4) for i in range(4)]).astype(F32)

    parts = blocks(sources, weight)
    pieces = [
        parts[0],
        lax.ppermute(parts[1], "c", CORE),
        lax.ppermute(parts[2], X_AXES, inverse(there)),
        lax.ppermute(parts[3], X_AXES, inverse(across)),
    ]

    up_total = up_part(idx, tokens, lows, grads, parts[0]).reshape(8, 8, KEYS)
    up_total = jnp.sum(lax.all_to_all(up_total, ("y", "c"), 0, 0, tiled=True), axis=0)

    slabs = mine.reshape(RANK // 4, SHARDS, HALF).transpose(1, 0, 2)
    up_total = jnp.broadcast_to(up_total[None], (SHARDS,) + up_total.shape)
    slabs = jnp.concatenate([slabs, up_total], axis=1).astype(BF)
    slabs, pieces[2] = lax.optimization_barrier((slabs, pieces[2]))
    slabs = lax.all_to_all(slabs, SHARD_AXES, 0, 0, tiled=True)
    slabs = jnp.sum(slabs.astype(F32), axis=0).astype(BF)
    slabs, pieces[3] = lax.optimization_barrier((slabs, pieces[3]))
    slabs = jnp.broadcast_to(slabs[None], (16,) + slabs.shape)
    slabs = lax.all_to_all(slabs, DP_AXES, 0, 0, tiled=True).astype(F32)
    slabs = slabs.reshape(2, 4, 2, RANK // 4 + 8, KEYS)
    factor = SCALE / jnp.sqrt(jnp.float32(TOKENS))
    slabs = factor * (slabs[0] + slabs[1])
    grad_down = slabs[:, :, : RANK // 4].transpose(1, 3, 0, 2).reshape(2 * HALF, RANK)
    grad_up = slabs[:, :, RANK // 4 :].reshape(RANK, KEYS)

    grad_tokens = assemble(idx, pieces, 0, NZ, [])
    return grad_tokens, grad_down, grad_up


def solution(mesh):
    fine = Mesh(mesh.devices.reshape(2, 4, 2, 2, 8), ("xh", "y", "c", "xl", "z"))
    everything = DP_AXES + SHARD_AXES
    in_specs = (
        P(everything, None),
        P(everything, None),
        P(DP_AXES, SHARD_AXES),
        P(SHARD_AXES, None),
        P(SHARD_AXES, None),
        P(),
        P(SHARD_AXES, None),
        P(),
    )
    out_specs = (P(everything, None), P(SHARD_AXES, None), P())
    return jax.shard_map(on_device, mesh=fine, in_specs=in_specs, out_specs=out_specs, check_vma=False)
```

```python
import functools

import jax
import jax.numpy as jnp
from jax import lax
from jax.experimental import pallas as pl
from jax.experimental.pallas import tpu as pltpu
from jax.sharding import Mesh, PartitionSpec as P

HEAD = 128
RANK = 64
BLOCK = 64
WIDTH = 16384
KEYS = 512
ROWS = 160
SHARDS = 16
NZ = 8
HALF = 512
LANES = 128
IDS = 16
ROPE_BASE = 500000.0
SCALE = 16.0 / RANK
TOKENS = 40960

BF = jnp.bfloat16
F32 = jnp.float32

X_AXES = ("xh", "c", "xl")
SHARD_AXES = ("xl", "z")
DP_AXES = ("xh", "y", "c")


BRIEF = pl.CostEstimate(flops=1, bytes_accessed=1, transcendentals=0)


def params(mib):
    return pltpu.CompilerParams(vmem_limit_bytes=mib * 1024 * 1024)


def dot(a, b, ca, cb):
    return lax.dot_general(a, b, (((ca,), (cb,)), ((), ())), preferred_element_type=F32)


def weight_kernel(idx, levels, scales, second, down, up, eighth, ids, weight, packet):
    for k in range(SHARDS):
        packet[k, :RANK, :] = eighth[...]
        packet[k, RANK:, :] = ids[...]
    scale = scales[...].astype(F32)
    n = HALF // BLOCK
    scale = jnp.where(idx[0] == 0, scale[:n], scale[n:])
    rows = []
    for j in range(n):
        level = levels[j * BLOCK : (j + 1) * BLOCK, :].astype(F32)
        rows.append((level * scale[j : j + 1]) * second[...])
    base = dot(up[...], down[...], 0, 0) * SCALE
    weight[...] = (jnp.concatenate(rows, axis=0).T + base).astype(BF)


def local_weight(idx, levels, scales, second, down, up, ids):
    full = lambda shape: pl.BlockSpec(shape, lambda i, s: (0,) * len(shape))
    return pl.pallas_call(
        weight_kernel,
        grid_spec=pltpu.PrefetchScalarGridSpec(
            num_scalar_prefetch=1,
            grid=(1,),
            in_specs=[
                pl.BlockSpec((HALF, KEYS), lambda i, s: (s[0], 0)),
                full(scales.shape),
                full((1, KEYS)),
                pl.BlockSpec((RANK, HALF), lambda i, s: (0, s[0])),
                full((RANK, KEYS)),
                pl.BlockSpec((RANK, LANES), lambda i, s: (0, s[0] * 4 + s[4])),
                full((IDS, LANES)),
            ],
            out_specs=[full((KEYS, HALF)), full((SHARDS, RANK + IDS, LANES))],
        ),
        out_shape=[
            jax.ShapeDtypeStruct((KEYS, HALF), BF),
            jax.ShapeDtypeStruct((SHARDS, RANK + IDS, LANES), BF),
        ],
        compiler_params=params(56),
        cost_estimate=BRIEF,
        name="weight",
    )(idx, levels, scales, second, down, up, down, ids)


def grads_kernel(idx, everyone, own, rotated, freqs, up, grads, low):
    mine = own[...]
    count = jnp.zeros((ROWS, LANES), F32)
    for k in range(SHARDS):
        for r in range(2):
            row = everyone[k, r : r + 1, :].astype(F32)
            count = count + jnp.where(row < mine, 1.0, 0.0)
    first = jnp.sum(count, axis=1, keepdims=True)
    place = lax.broadcasted_iota(jnp.int32, (ROWS, 1), 0) + idx[3] * ROWS
    position = place.astype(F32) - first
    angle = position * freqs[...]
    cosine = jnp.cos(angle)
    lane = lax.broadcasted_iota(jnp.int32, (ROWS, HEAD), 1)
    sine = jnp.where(lane < HEAD // 2, 1.0, -1.0) * jnp.sin(angle)
    for h in range(KEYS // HEAD):
        cols = slice(h * HEAD, (h + 1) * HEAD)
        g = rotated[:, cols].astype(F32)
        grads[:, cols] = (g * cosine + pltpu.roll(g, HEAD // 2, 1) * sine).astype(BF)
    low[...] = dot(up[...], grads[...], 1, 1).astype(BF)


def make_grads(idx, everyone, own, rotated, freqs, up):
    full = lambda shape: pl.BlockSpec(shape, lambda i, s: (0,) * len(shape))
    return pl.pallas_call(
        grads_kernel,
        grid_spec=pltpu.PrefetchScalarGridSpec(
            num_scalar_prefetch=1,
            grid=(1,),
            in_specs=[
                pl.BlockSpec((SHARDS, IDS, LANES), lambda i, s: (0, RANK // IDS, 0)),
                full((ROWS, 1)),
                full((ROWS, KEYS)),
                full((1, HEAD)),
                full((RANK, KEYS)),
            ],
            out_specs=[full((ROWS, KEYS)), full((RANK, ROWS))],
        ),
        out_shape=[jax.ShapeDtypeStruct((ROWS, KEYS), BF), jax.ShapeDtypeStruct((RANK, ROWS), BF)],
        compiler_params=params(56),
        cost_estimate=BRIEF,
        name="grads",
    )(idx, everyone, own, rotated, freqs, up)


CHUNKS = 8
WIDE = WIDTH // CHUNKS
STEP = WIDE // (2 * HALF)


def down_kernel(idx, low, tokens, *refs):
    keep, send, (held, keep_held, send_held, sems) = refs[:2], refs[2:4], refs[4:]
    c, x = idx[0], idx[2]
    loads = [
        pltpu.make_async_copy(tokens.at[:, pl.ds(i * WIDE, WIDE)], held.at[i], sems.at[i]) for i in range(CHUNKS)
    ]
    for load in loads:
        load.start()
    stores = []
    for i in range(CHUNKS):
        loads[i].wait()
        for k in range(STEP):
            at = (i * STEP + k) * HALF
            mine = pl.multiple_of(k * 2 * HALF + c * HALF, HALF)
            other = pl.multiple_of(k * 2 * HALF + (1 - c) * HALF, HALF)
            send_held[:, at : at + HALF] = dot(low[...], held[i, :, pl.ds(other, HALF)], 1, 0).astype(BF)
            keep_held[:, at : at + HALF] = dot(low[...], held[i, :, pl.ds(mine, HALF)], 1, 0)
    for d in range(2):
        half = WIDTH // 4
        cols = pl.ds(pl.multiple_of(lax.rem(x + d, 2) * half, half), half)
        for source, target in ((send_held, send[d]), (keep_held, keep[d])):
            stores.append(pltpu.make_async_copy(source.at[:, cols], target, sems.at[CHUNKS + len(stores)]))
            stores[-1].start()
    for store in stores:
        store.wait()


def down_part(idx, low, tokens):
    anywhere = pl.BlockSpec(memory_space=pl.ANY)
    return pl.pallas_call(
        down_kernel,
        in_specs=[pl.BlockSpec(memory_space=pltpu.SMEM), pl.BlockSpec(memory_space=pltpu.VMEM), anywhere],
        out_specs=[anywhere] * 4,
        out_shape=[jax.ShapeDtypeStruct((RANK, WIDTH // 4), dtype) for dtype in (F32, F32, BF, BF)],
        scratch_shapes=[
            pltpu.VMEM((CHUNKS, ROWS, WIDE), BF),
            pltpu.VMEM((RANK, WIDTH // 2), F32),
            pltpu.VMEM((RANK, WIDTH // 2), BF),
            pltpu.SemaphoreType.DMA((CHUNKS + 4,)),
        ],
        compiler_params=params(56),
        cost_estimate=BRIEF,
        name="down",
    )(idx, low, tokens)


def up_kernel(idx, tokens, *refs):
    given, (grads, out, held, lows, sems) = refs[:2], refs[2:]
    c = idx[0]
    loads = [
        pltpu.make_async_copy(tokens.at[:, pl.ds(i * WIDE, WIDE)], held.at[i], sems.at[i]) for i in range(CHUNKS)
    ]
    pieces = [pltpu.make_async_copy(p, lows.at[k], sems.at[CHUNKS + k]) for k, p in enumerate(given)]
    for copy in pieces + loads:
        copy.start()
    for copy in pieces:
        copy.wait()
    total = jnp.zeros((ROWS, RANK), F32)
    for i in range(CHUNKS):
        loads[i].wait()
        for k in range(STEP):
            for p in range(2):
                h = c if p == 0 else 1 - c
                at = pl.multiple_of(k * 2 * HALF + h * HALF, HALF)
                rows = jnp.concatenate([lows[p, q, i * STEP + k] for q in range(4)], axis=1)
                total = total + dot(held[i, :, pl.ds(at, HALF)], rows, 1, 1)
    product = dot(total.astype(BF), grads[...], 0, 0).astype(BF)
    for k in range(8):
        half = (k // 2) % 2 * (KEYS // 2)
        out[k] = product[:, half : half + KEYS // 2]


def up_part(idx, tokens, lows, grads):
    anywhere = pl.BlockSpec(memory_space=pl.ANY)
    return pl.pallas_call(
        up_kernel,
        in_specs=[pl.BlockSpec(memory_space=pltpu.SMEM)]
        + [anywhere] * 3
        + [pl.BlockSpec(memory_space=pltpu.VMEM)],
        out_specs=pl.BlockSpec(memory_space=pltpu.VMEM),
        out_shape=jax.ShapeDtypeStruct((8, RANK, KEYS // 2), BF),
        scratch_shapes=[
            pltpu.VMEM((CHUNKS, ROWS, WIDE), BF),
            pltpu.VMEM((2, 4, SHARDS, RANK, LANES), BF),
            pltpu.SemaphoreType.DMA((CHUNKS + 2,)),
        ],
        compiler_params=params(56),
        cost_estimate=BRIEF,
        name="up",
    )(idx, tokens, *lows, grads)


def block_kernel(own, core, there, across, weight, after, o0, o1, o2, o3, rows, held, made, sems):
    loads = [
        pltpu.make_async_copy(weight.at[pl.ds(i * KEYS, KEYS), :], held.at[i], sems.at[4 * NZ + i]) for i in range(NZ)
    ]
    for load in loads:
        load.start()
    for k, source in enumerate((own, core, there, across)):
        rows[k * ROWS : (k + 1) * ROWS, :] = source[...]
    stores = []
    for i in range(NZ):
        loads[i].wait()
        made[i] = dot(rows[...], held[i], 1, 0).astype(BF)
        for k, out in enumerate((o0, o1, o2, o3)):
            stores.append(
                pltpu.make_async_copy(
                    made.at[i, pl.ds(k * ROWS, ROWS), :],
                    out.at[:, pl.ds(i * HALF, HALF)],
                    sems.at[4 * i + k],
                )
            )
            stores[-1].start()
    for store in stores:
        store.wait()


def blocks(sources, weight, after):
    anywhere = pl.BlockSpec(memory_space=pl.ANY)
    return pl.pallas_call(
        block_kernel,
        in_specs=[pl.BlockSpec(memory_space=pltpu.VMEM)] * 4 + [anywhere] * 2,
        out_specs=[anywhere] * 4,
        out_shape=[jax.ShapeDtypeStruct((ROWS, NZ * HALF), BF)] * 4,
        scratch_shapes=[
            pltpu.VMEM((4 * ROWS, KEYS), BF),
            pltpu.VMEM((NZ, KEYS, HALF), BF),
            pltpu.VMEM((NZ, 4 * ROWS, HALF), BF),
            pltpu.SemaphoreType.DMA((5 * NZ,)),
        ],
        compiler_params=params(56),
        cost_estimate=BRIEF,
        name="blocks",
    )(*sources, weight, after)


def assemble_kernel(places, idx, *refs):
    out, sems = refs[-2:]
    copies = []
    for k, piece in zip(places, refs):
        x = idx[2] if k < 2 else 1 - idx[2]
        h = idx[0] if k % 2 == 0 else 1 - idx[0]
        for j in range(NZ):
            col = pl.multiple_of(((x * NZ + j) * 2 + h) * HALF, HALF)
            copies.append(
                pltpu.make_async_copy(
                    piece.at[:, pl.ds(j * HALF, HALF)],
                    out.at[:, pl.ds(col, HALF)],
                    sems.at[len(copies)],
                )
            )
    for copy in copies:
        copy.start()
    for copy in copies:
        copy.wait()


def assemble(idx, places, pieces, before):
    anywhere = pl.BlockSpec(memory_space=pl.ANY)
    return pl.pallas_call(
        functools.partial(assemble_kernel, places),
        in_specs=[pl.BlockSpec(memory_space=pltpu.SMEM)]
        + [pl.BlockSpec(memory_space=pltpu.VMEM)] * len(pieces)
        + [anywhere] * len(before),
        out_specs=anywhere,
        scratch_shapes=[pltpu.SemaphoreType.DMA((NZ * len(pieces),))],
        out_shape=jax.ShapeDtypeStruct((ROWS, WIDTH), BF),
        input_output_aliases={1 + len(pieces): 0} if before else {},
        compiler_params=params(8),
        cost_estimate=BRIEF,
        name="assemble",
    )(idx, *pieces, *before)


def x_permutation(swap):
    at = lambda x, c: ((x // 2) * 2 + c) * 2 + x % 2
    pairs = []
    for x in range(4):
        for c in range(2):
            if (c ^ swap) == 0:
                pairs.append((at(x, c), at((x + 1) % 4, 0)))
            else:
                pairs.append((at(x, c), at((x - 1) % 4, 1)))
    return pairs


def inverse(pairs):
    return [(b, a) for a, b in pairs]


CORE = [(0, 1), (1, 0)]


def on_device(tokens, rotated, documents, levels, scales, second, down, up):
    xh, y, c, xl, z = (lax.axis_index(a) for a in ("xh", "y", "c", "xl", "z"))
    idx = jnp.stack([c, xh, xl, xl * NZ + z, y]).astype(jnp.int32)

    ids = jnp.pad(documents.astype(BF), ((0, 0), (0, 2 * LANES - ROWS)), constant_values=1000.0)
    ids = jnp.pad(ids.reshape(2, LANES), ((0, IDS - 2), (0, 0)))
    weight, packet = local_weight(idx, levels, scales, second, down.T, up, ids)
    weight = lax.all_gather(weight, "z", tiled=True)
    everyone = lax.all_to_all(packet, SHARD_AXES, 0, 0, tiled=True)

    half = HEAD // 2
    freqs = ROPE_BASE ** (-jnp.arange(half, dtype=F32) * 2.0 / HEAD)
    freqs = jnp.concatenate([freqs, freqs])[None, :]
    own = documents.astype(F32).reshape(ROWS, 1)
    grads, low = make_grads(idx, everyone, own, rotated, freqs, up)

    there, across = x_permutation(0), x_permutation(1)
    sources = [
        grads,
        lax.ppermute(grads, "c", CORE),
        lax.ppermute(grads, X_AXES, there),
        lax.ppermute(grads, X_AXES, across),
    ]

    made = down_part(idx, low, tokens)
    keep, send = made[:2], made[2:]
    sent = [lax.ppermute(part, "c", CORE) for part in send]

    lows = jnp.broadcast_to(everyone[None, :, :RANK], (4, SHARDS, RANK, LANES))
    lows = lax.all_to_all(lows, "y", 0, 0, tiled=True)
    lows, sent = lax.optimization_barrier((lows, sent))
    lows = [lows, lax.ppermute(lows, "c", CORE)]

    halves = [(a + b.astype(F32)).reshape(2, RANK // 2, WIDTH // 4) for a, b in zip(keep, sent)]
    own_half = lax.dynamic_index_in_dim(halves[0], xh, 0, keepdims=False)
    parcels = [
        lax.dynamic_index_in_dim(half, at, 0, keepdims=False).astype(BF)
        for half, at in ((halves[0], 1 - xh), (halves[1], xh), (halves[1], 1 - xh))
    ]
    parcels, sources[1:] = lax.optimization_barrier((parcels, sources[1:]))
    parcels = [
        lax.ppermute(parcel, ("xh", "xl"), [(i, i ^ bits) for i in range(4)])
        for parcel, bits in zip(parcels, (2, 1, 3))
    ]

    up_total = up_part(idx, tokens, lows, grads)
    parts = blocks(sources, weight, up_total)
    pieces = [
        parts[0],
        lax.ppermute(parts[1], "c", CORE),
        lax.ppermute(parts[2], X_AXES, inverse(there)),
        lax.ppermute(parts[3], X_AXES, inverse(across)),
    ]

    up_total = lax.all_to_all(up_total, X_AXES, 0, 0, tiled=True)
    parcels, up_total, _ = lax.optimization_barrier((parcels, up_total, parts[0]))
    up_total = jnp.sum(up_total.astype(F32), axis=0).reshape(4, RANK // 8, KEYS)
    total = own_half + parcels[0].astype(F32) + parcels[1].astype(F32) + parcels[2].astype(F32)
    total = jnp.concatenate([total.reshape(4, RANK // 8, WIDTH // 4), up_total], axis=2)
    mine = lax.dynamic_index_in_dim(total, y, 0, keepdims=False)
    for d in (1, 3, 2):
        out = lax.dynamic_index_in_dim(total, (y + d) % 4, 0, keepdims=False).astype(BF)
        mine = mine + lax.ppermute(out, "y", [(i, (i + d) % 4) for i in range(4)]).astype(F32)
    total = mine.astype(BF)

    slabs = total[:, : WIDTH // 4].reshape(RANK // 8, NZ, HALF).transpose(1, 0, 2)
    up_total = jnp.broadcast_to(total[None, :, WIDTH // 4 :], (NZ, RANK // 8, KEYS))
    slabs = jnp.concatenate([slabs, up_total], axis=1)
    slabs = lax.all_to_all(slabs, "z", 0, 0, tiled=True)
    slabs = jnp.sum(slabs.astype(F32), axis=0).astype(BF)
    slabs, pieces[2] = lax.optimization_barrier((slabs, pieces[2]))
    slabs = jnp.broadcast_to(slabs[None], (16,) + slabs.shape)
    slabs = lax.all_to_all(slabs, DP_AXES, 0, 0, tiled=True).astype(F32)
    factor = SCALE / jnp.sqrt(jnp.float32(TOKENS))
    slabs = factor * slabs.reshape(2, 4, 2, RANK // 4, KEYS)
    grad_down = slabs[:, :, :, : RANK // 8].transpose(2, 4, 0, 1, 3).reshape(2 * HALF, RANK)
    grad_up = slabs[0, :, :, RANK // 8 :].reshape(4, 2, RANK // 4, KEYS // 2)
    grad_up = grad_up.transpose(0, 2, 1, 3).reshape(RANK, KEYS)

    grad_tokens = assemble(idx, (0, 1, 2), pieces[:3], [])
    grad_tokens = assemble(idx, (3,), pieces[3:], [grad_tokens])
    return grad_tokens, grad_down, grad_up


def solution(mesh):
    fine = Mesh(mesh.devices.reshape(2, 4, 2, 2, 8), ("xh", "y", "c", "xl", "z"))
    everything = DP_AXES + SHARD_AXES
    in_specs = (
        P(everything, None),
        P(everything, None),
        P(DP_AXES, SHARD_AXES),
        P(SHARD_AXES, None),
        P(SHARD_AXES, None),
        P(),
        P(SHARD_AXES, None),
        P(),
    )
    out_specs = (P(everything, None), P(SHARD_AXES, None), P())
    return jax.shard_map(on_device, mesh=fine, in_specs=in_specs, out_specs=out_specs, check_vma=False)
```

```python
import functools

import jax
import jax.numpy as jnp
from jax import lax
from jax.experimental import pallas as pl
from jax.experimental.pallas import tpu as pltpu
from jax.sharding import Mesh, PartitionSpec as P

HEAD = 128
RANK = 64
BLOCK = 64
WIDTH = 16384
KEYS = 512
ROWS = 160
SHARDS = 16
NZ = 8
HALF = 512
LANES = 128
IDS = 16
ROPE_BASE = 500000.0
SCALE = 16.0 / RANK
TOKENS = 40960

BF = jnp.bfloat16
F32 = jnp.float32

X_AXES = ("xh", "c", "xl")
SHARD_AXES = ("xl", "z")
DP_AXES = ("xh", "y", "c")


BRIEF = pl.CostEstimate(flops=1, bytes_accessed=1, transcendentals=0)


def params(mib):
    return pltpu.CompilerParams(vmem_limit_bytes=mib * 1024 * 1024)


def dot(a, b, ca, cb):
    return lax.dot_general(a, b, (((ca,), (cb,)), ((), ())), preferred_element_type=F32)


def weight_kernel(idx, levels, scales, second, down, up, eighth, ids, weight, packet):
    for k in range(SHARDS):
        packet[k, :RANK, :] = eighth[...]
        packet[k, RANK:, :] = ids[...]
    scale = scales[...].astype(F32)
    n = HALF // BLOCK
    scale = jnp.where(idx[0] == 0, scale[:n], scale[n:])
    rows = []
    for j in range(n):
        level = levels[j * BLOCK : (j + 1) * BLOCK, :].astype(F32)
        rows.append((level * scale[j : j + 1]) * second[...])
    base = dot(up[...], down[...], 0, 0) * SCALE
    weight[...] = (jnp.concatenate(rows, axis=0).T + base).astype(BF)


def local_weight(idx, levels, scales, second, down, up, ids):
    full = lambda shape: pl.BlockSpec(shape, lambda i, s: (0,) * len(shape))
    return pl.pallas_call(
        weight_kernel,
        grid_spec=pltpu.PrefetchScalarGridSpec(
            num_scalar_prefetch=1,
            grid=(1,),
            in_specs=[
                pl.BlockSpec((HALF, KEYS), lambda i, s: (s[0], 0)),
                full(scales.shape),
                full((1, KEYS)),
                pl.BlockSpec((RANK, HALF), lambda i, s: (0, s[0])),
                full((RANK, KEYS)),
                pl.BlockSpec((RANK, LANES), lambda i, s: (0, s[0] * 4 + s[4])),
                full((IDS, LANES)),
            ],
            out_specs=[full((KEYS, HALF)), full((SHARDS, RANK + IDS, LANES))],
        ),
        out_shape=[
            jax.ShapeDtypeStruct((KEYS, HALF), BF),
            jax.ShapeDtypeStruct((SHARDS, RANK + IDS, LANES), BF),
        ],
        compiler_params=params(56),
        cost_estimate=BRIEF,
        name="weight",
    )(idx, levels, scales, second, down, up, down, ids)


def grads_kernel(idx, everyone, own, rotated, freqs, up, grads, low):
    mine = own[...]
    count = jnp.zeros((ROWS, LANES), F32)
    for k in range(SHARDS):
        for r in range(2):
            row = everyone[k, r : r + 1, :].astype(F32)
            count = count + jnp.where(row < mine, 1.0, 0.0)
    first = jnp.sum(count, axis=1, keepdims=True)
    place = lax.broadcasted_iota(jnp.int32, (ROWS, 1), 0) + idx[3] * ROWS
    position = place.astype(F32) - first
    angle = position * freqs[...]
    cosine = jnp.cos(angle)
    lane = lax.broadcasted_iota(jnp.int32, (ROWS, HEAD), 1)
    sine = jnp.where(lane < HEAD // 2, 1.0, -1.0) * jnp.sin(angle)
    for h in range(KEYS // HEAD):
        cols = slice(h * HEAD, (h + 1) * HEAD)
        g = rotated[:, cols].astype(F32)
        grads[:, cols] = (g * cosine + pltpu.roll(g, HEAD // 2, 1) * sine).astype(BF)
    low[...] = dot(up[...], grads[...], 1, 1).astype(BF)


def make_grads(idx, everyone, own, rotated, freqs, up):
    full = lambda shape: pl.BlockSpec(shape, lambda i, s: (0,) * len(shape))
    return pl.pallas_call(
        grads_kernel,
        grid_spec=pltpu.PrefetchScalarGridSpec(
            num_scalar_prefetch=1,
            grid=(1,),
            in_specs=[
                pl.BlockSpec((SHARDS, IDS, LANES), lambda i, s: (0, RANK // IDS, 0)),
                full((ROWS, 1)),
                full((ROWS, KEYS)),
                full((1, HEAD)),
                full((RANK, KEYS)),
            ],
            out_specs=[full((ROWS, KEYS)), full((RANK, ROWS))],
        ),
        out_shape=[jax.ShapeDtypeStruct((ROWS, KEYS), BF), jax.ShapeDtypeStruct((RANK, ROWS), BF)],
        compiler_params=params(56),
        cost_estimate=BRIEF,
        name="grads",
    )(idx, everyone, own, rotated, freqs, up)


CHUNKS = 8
WIDE = WIDTH // CHUNKS
STEP = WIDE // (2 * HALF)


def down_kernel(idx, low, tokens, *refs):
    keep, send, (held, keep_held, send_held, sems) = refs[:2], refs[2:4], refs[4:]
    c, x = idx[0], idx[2]
    loads = [
        pltpu.make_async_copy(tokens.at[:, pl.ds(i * WIDE, WIDE)], held.at[i], sems.at[i]) for i in range(CHUNKS)
    ]
    for load in loads:
        load.start()
    stores = []
    for i in range(CHUNKS):
        loads[i].wait()
        for k in range(STEP):
            at = (i * STEP + k) * HALF
            mine = pl.multiple_of(k * 2 * HALF + c * HALF, HALF)
            other = pl.multiple_of(k * 2 * HALF + (1 - c) * HALF, HALF)
            send_held[:, at : at + HALF] = dot(low[...], held[i, :, pl.ds(other, HALF)], 1, 0).astype(BF)
            keep_held[:, at : at + HALF] = dot(low[...], held[i, :, pl.ds(mine, HALF)], 1, 0)
    for d in range(2):
        half = WIDTH // 4
        cols = pl.ds(pl.multiple_of(lax.rem(x + d, 2) * half, half), half)
        for source, target in ((send_held, send[d]), (keep_held, keep[d])):
            stores.append(pltpu.make_async_copy(source.at[:, cols], target, sems.at[CHUNKS + len(stores)]))
            stores[-1].start()
    for store in stores:
        store.wait()


def down_part(idx, low, tokens):
    anywhere = pl.BlockSpec(memory_space=pl.ANY)
    return pl.pallas_call(
        down_kernel,
        in_specs=[pl.BlockSpec(memory_space=pltpu.SMEM), pl.BlockSpec(memory_space=pltpu.VMEM), anywhere],
        out_specs=[anywhere] * 4,
        out_shape=[jax.ShapeDtypeStruct((RANK, WIDTH // 4), dtype) for dtype in (F32, F32, BF, BF)],
        scratch_shapes=[
            pltpu.VMEM((CHUNKS, ROWS, WIDE), BF),
            pltpu.VMEM((RANK, WIDTH // 2), F32),
            pltpu.VMEM((RANK, WIDTH // 2), BF),
            pltpu.SemaphoreType.DMA((CHUNKS + 4,)),
        ],
        compiler_params=params(56),
        cost_estimate=BRIEF,
        name="down",
    )(idx, low, tokens)


def up_kernel(idx, tokens, *refs):
    given, (grads, out, held, lows, sems) = refs[:2], refs[2:]
    c = idx[0]
    loads = [
        pltpu.make_async_copy(tokens.at[:, pl.ds(i * WIDE, WIDE)], held.at[i], sems.at[i]) for i in range(CHUNKS)
    ]
    pieces = [pltpu.make_async_copy(p, lows.at[k], sems.at[CHUNKS + k]) for k, p in enumerate(given)]
    for copy in pieces + loads:
        copy.start()
    for copy in pieces:
        copy.wait()
    total = jnp.zeros((ROWS, RANK), F32)
    for i in range(CHUNKS):
        loads[i].wait()
        for k in range(STEP):
            for p in range(2):
                h = c if p == 0 else 1 - c
                at = pl.multiple_of(k * 2 * HALF + h * HALF, HALF)
                rows = jnp.concatenate([lows[p, q, i * STEP + k] for q in range(4)], axis=1)
                total = total + dot(held[i, :, pl.ds(at, HALF)], rows, 1, 1)
    product = dot(total.astype(BF), grads[...], 0, 0).astype(BF)
    for k in range(8):
        half = (k // 2) % 2 * (KEYS // 2)
        out[k] = product[:, half : half + KEYS // 2]


def up_part(idx, tokens, lows, grads):
    anywhere = pl.BlockSpec(memory_space=pl.ANY)
    return pl.pallas_call(
        up_kernel,
        in_specs=[pl.BlockSpec(memory_space=pltpu.SMEM)]
        + [anywhere] * 3
        + [pl.BlockSpec(memory_space=pltpu.VMEM)],
        out_specs=pl.BlockSpec(memory_space=pltpu.VMEM),
        out_shape=jax.ShapeDtypeStruct((8, RANK, KEYS // 2), BF),
        scratch_shapes=[
            pltpu.VMEM((CHUNKS, ROWS, WIDE), BF),
            pltpu.VMEM((2, 4, SHARDS, RANK, LANES), BF),
            pltpu.SemaphoreType.DMA((CHUNKS + 2,)),
        ],
        compiler_params=params(56),
        cost_estimate=BRIEF,
        name="up",
    )(idx, tokens, *lows, grads)


def block_kernel(first, second, weight, after, o0, o1, rows, held, made, sems):
    loads = [
        pltpu.make_async_copy(weight.at[pl.ds(i * KEYS, KEYS), :], held.at[i], sems.at[2 * NZ + i]) for i in range(NZ)
    ]
    for load in loads:
        load.start()
    rows[:ROWS, :] = first[...]
    rows[ROWS:, :] = second[...]
    stores = []
    for i in range(NZ):
        loads[i].wait()
        made[i] = dot(rows[...], held[i], 1, 0).astype(BF)
        for k, out in enumerate((o0, o1)):
            stores.append(
                pltpu.make_async_copy(
                    made.at[i, pl.ds(k * ROWS, ROWS), :],
                    out.at[:, pl.ds(i * HALF, HALF)],
                    sems.at[2 * i + k],
                )
            )
            stores[-1].start()
    for store in stores:
        store.wait()


def blocks(sources, weight, after):
    anywhere = pl.BlockSpec(memory_space=pl.ANY)
    return pl.pallas_call(
        block_kernel,
        in_specs=[pl.BlockSpec(memory_space=pltpu.VMEM)] * 2 + [anywhere] * 2,
        out_specs=[anywhere] * 2,
        out_shape=[jax.ShapeDtypeStruct((ROWS, NZ * HALF), BF)] * 2,
        scratch_shapes=[
            pltpu.VMEM((2 * ROWS, KEYS), BF),
            pltpu.VMEM((NZ, KEYS, HALF), BF),
            pltpu.VMEM((NZ, 2 * ROWS, HALF), BF),
            pltpu.SemaphoreType.DMA((3 * NZ,)),
        ],
        compiler_params=params(56),
        cost_estimate=BRIEF,
        name="blocks",
    )(*sources, weight, after)


def assemble_kernel(places, idx, *refs):
    out, sems = refs[-2:]
    copies = []
    for k, piece in zip(places, refs):
        x = idx[2] if k < 2 else 1 - idx[2]
        h = idx[0] if k % 2 == 0 else 1 - idx[0]
        for j in range(NZ):
            col = pl.multiple_of(((x * NZ + j) * 2 + h) * HALF, HALF)
            copies.append(
                pltpu.make_async_copy(
                    piece.at[:, pl.ds(j * HALF, HALF)],
                    out.at[:, pl.ds(col, HALF)],
                    sems.at[len(copies)],
                )
            )
    for copy in copies:
        copy.start()
    for copy in copies:
        copy.wait()


def assemble(idx, places, pieces, before):
    anywhere = pl.BlockSpec(memory_space=pl.ANY)
    return pl.pallas_call(
        functools.partial(assemble_kernel, places),
        in_specs=[pl.BlockSpec(memory_space=pltpu.SMEM)]
        + [pl.BlockSpec(memory_space=pltpu.VMEM)] * len(pieces)
        + [anywhere] * len(before),
        out_specs=anywhere,
        scratch_shapes=[pltpu.SemaphoreType.DMA((NZ * len(pieces),))],
        out_shape=jax.ShapeDtypeStruct((ROWS, WIDTH), BF),
        input_output_aliases={1 + len(pieces): 0} if before else {},
        compiler_params=params(8),
        cost_estimate=BRIEF,
        name="assemble",
    )(idx, *pieces, *before)


def x_permutation(swap):
    at = lambda x, c: ((x // 2) * 2 + c) * 2 + x % 2
    pairs = []
    for x in range(4):
        for c in range(2):
            if (c ^ swap) == 0:
                pairs.append((at(x, c), at((x + 1) % 4, 0)))
            else:
                pairs.append((at(x, c), at((x - 1) % 4, 1)))
    return pairs


def inverse(pairs):
    return [(b, a) for a, b in pairs]


CORE = [(0, 1), (1, 0)]


def on_device(tokens, rotated, documents, levels, scales, second, down, up):
    xh, y, c, xl, z = (lax.axis_index(a) for a in ("xh", "y", "c", "xl", "z"))
    idx = jnp.stack([c, xh, xl, xl * NZ + z, y]).astype(jnp.int32)

    ids = jnp.pad(documents.astype(BF), ((0, 0), (0, 2 * LANES - ROWS)), constant_values=1000.0)
    ids = jnp.pad(ids.reshape(2, LANES), ((0, IDS - 2), (0, 0)))
    weight, packet = local_weight(idx, levels, scales, second, down.T, up, ids)
    weight = lax.all_gather(weight, "z", tiled=True)
    everyone = lax.all_to_all(packet, SHARD_AXES, 0, 0, tiled=True)

    half = HEAD // 2
    freqs = ROPE_BASE ** (-jnp.arange(half, dtype=F32) * 2.0 / HEAD)
    freqs = jnp.concatenate([freqs, freqs])[None, :]
    own = documents.astype(F32).reshape(ROWS, 1)
    grads, low = make_grads(idx, everyone, own, rotated, freqs, up)

    there, across = x_permutation(0), x_permutation(1)
    sources = [
        grads,
        lax.ppermute(grads, "c", CORE),
        lax.ppermute(grads, X_AXES, there),
        lax.ppermute(grads, X_AXES, across),
    ]

    made = down_part(idx, low, tokens)
    keep, send = made[:2], made[2:]
    sent = [lax.ppermute(part, "c", CORE) for part in send]

    lows = jnp.broadcast_to(everyone[None, :, :RANK], (4, SHARDS, RANK, LANES))
    lows = lax.all_to_all(lows, "y", 0, 0, tiled=True)
    lows, sent = lax.optimization_barrier((lows, sent))
    lows = [lows, lax.ppermute(lows, "c", CORE)]

    halves = [(a + b.astype(F32)).reshape(2, RANK // 2, WIDTH // 4) for a, b in zip(keep, sent)]
    own_half = lax.dynamic_index_in_dim(halves[0], xh, 0, keepdims=False)
    parcels = [
        lax.dynamic_index_in_dim(half, at, 0, keepdims=False).astype(BF)
        for half, at in ((halves[0], 1 - xh), (halves[1], xh), (halves[1], 1 - xh))
    ]
    parcels, sources[1:] = lax.optimization_barrier((parcels, sources[1:]))
    parcels = [
        lax.ppermute(parcel, ("xh", "xl"), [(i, i ^ bits) for i in range(4)])
        for parcel, bits in zip(parcels, (2, 1, 3))
    ]

    up_total = up_part(idx, tokens, lows, grads)
    away = blocks(sources[2:], weight, up_total)
    here = blocks(sources[:2], weight, away[0])
    pieces = [
        here[0],
        lax.ppermute(here[1], "c", CORE),
        lax.ppermute(away[0], X_AXES, inverse(there)),
        lax.ppermute(away[1], X_AXES, inverse(across)),
    ]

    up_total = lax.all_to_all(up_total, X_AXES, 0, 0, tiled=True)
    parcels, up_total, _ = lax.optimization_barrier((parcels, up_total, away[0]))
    up_total = jnp.sum(up_total.astype(F32), axis=0).reshape(4, RANK // 8, KEYS)
    total = own_half + parcels[0].astype(F32) + parcels[1].astype(F32) + parcels[2].astype(F32)
    total = jnp.concatenate([total.reshape(4, RANK // 8, WIDTH // 4), up_total], axis=2)
    mine = lax.dynamic_index_in_dim(total, y, 0, keepdims=False)
    for d in (1, 3, 2):
        out = lax.dynamic_index_in_dim(total, (y + d) % 4, 0, keepdims=False).astype(BF)
        mine = mine + lax.ppermute(out, "y", [(i, (i + d) % 4) for i in range(4)]).astype(F32)
    total = mine.astype(BF)

    slabs = total[:, : WIDTH // 4].reshape(RANK // 8, NZ, HALF).transpose(1, 0, 2)
    up_total = jnp.broadcast_to(total[None, :, WIDTH // 4 :], (NZ, RANK // 8, KEYS))
    slabs = jnp.concatenate([slabs, up_total], axis=1)
    slabs, pieces[0] = lax.optimization_barrier((slabs, pieces[0]))
    slabs = lax.all_to_all(slabs, "z", 0, 0, tiled=True)
    slabs = jnp.sum(slabs.astype(F32), axis=0).astype(BF)
    slabs, pieces[2] = lax.optimization_barrier((slabs, pieces[2]))
    slabs = jnp.broadcast_to(slabs[None], (16,) + slabs.shape)
    slabs = lax.all_to_all(slabs, DP_AXES, 0, 0, tiled=True).astype(F32)
    factor = SCALE / jnp.sqrt(jnp.float32(TOKENS))
    slabs = factor * slabs.reshape(2, 4, 2, RANK // 4, KEYS)
    grad_down = slabs[:, :, :, : RANK // 8].transpose(2, 4, 0, 1, 3).reshape(2 * HALF, RANK)
    grad_up = slabs[0, :, :, RANK // 8 :].reshape(4, 2, RANK // 4, KEYS // 2)
    grad_up = grad_up.transpose(0, 2, 1, 3).reshape(RANK, KEYS)

    grad_tokens = assemble(idx, (0, 1, 2), pieces[:3], [])
    grad_tokens = assemble(idx, (3,), pieces[3:], [grad_tokens])
    return grad_tokens, grad_down, grad_up


def solution(mesh):
    fine = Mesh(mesh.devices.reshape(2, 4, 2, 2, 8), ("xh", "y", "c", "xl", "z"))
    everything = DP_AXES + SHARD_AXES
    in_specs = (
        P(everything, None),
        P(everything, None),
        P(DP_AXES, SHARD_AXES),
        P(SHARD_AXES, None),
        P(SHARD_AXES, None),
        P(),
        P(SHARD_AXES, None),
        P(),
    )
    out_specs = (P(everything, None), P(SHARD_AXES, None), P())
    return jax.shard_map(on_device, mesh=fine, in_specs=in_specs, out_specs=out_specs, check_vma=False)
```

```python
import functools

import jax
import jax.numpy as jnp
from jax import lax
from jax.experimental import pallas as pl
from jax.experimental.pallas import tpu as pltpu
from jax.sharding import Mesh, PartitionSpec as P

HEAD = 128
RANK = 64
BLOCK = 64
WIDTH = 16384
KEYS = 512
ROWS = 160
SHARDS = 16
NZ = 8
HALF = 512
LANES = 128
IDS = 16
ROPE_BASE = 500000.0
SCALE = 16.0 / RANK
TOKENS = 40960

BF = jnp.bfloat16
F32 = jnp.float32

X_AXES = ("xh", "c", "xl")
SHARD_AXES = ("xl", "z")
DP_AXES = ("xh", "y", "c")


BRIEF = pl.CostEstimate(flops=1, bytes_accessed=1, transcendentals=0)


def params(mib):
    return pltpu.CompilerParams(vmem_limit_bytes=mib * 1024 * 1024)


def dot(a, b, ca, cb):
    return lax.dot_general(a, b, (((ca,), (cb,)), ((), ())), preferred_element_type=F32)


def weight_kernel(idx, levels, scales, second, down, up, eighth, ids, weight, packet):
    row = lax.broadcasted_iota(jnp.int32, (IDS, LANES), 0)
    table = jnp.where(row == 0, ids[:, :LANES], ids[:, LANES:]).astype(F32).astype(BF)
    for k in range(SHARDS):
        packet[k, :RANK, :] = eighth[...]
        packet[k, RANK:, :] = table
    scale = scales[...].astype(F32)
    n = HALF // BLOCK
    scale = jnp.where(idx[0] == 0, scale[:n], scale[n:])
    rows = []
    for j in range(n):
        level = levels[j * BLOCK : (j + 1) * BLOCK, :].astype(F32)
        rows.append((level * scale[j : j + 1]) * second[...])
    base = dot(up[...], down[...], 0, 0) * SCALE
    weight[...] = (jnp.concatenate(rows, axis=0).T + base).astype(BF)


def local_weight(idx, levels, scales, second, down, up, ids):
    full = lambda shape: pl.BlockSpec(shape, lambda i, s: (0,) * len(shape))
    return pl.pallas_call(
        weight_kernel,
        grid_spec=pltpu.PrefetchScalarGridSpec(
            num_scalar_prefetch=1,
            grid=(1,),
            in_specs=[
                pl.BlockSpec((HALF, KEYS), lambda i, s: (s[0], 0)),
                full(scales.shape),
                full((1, KEYS)),
                pl.BlockSpec((RANK, HALF), lambda i, s: (0, s[0])),
                full((RANK, KEYS)),
                pl.BlockSpec((RANK, LANES), lambda i, s: (0, s[0] * 4 + s[4])),
                full((1, 2 * LANES)),
            ],
            out_specs=[full((KEYS, HALF)), full((SHARDS, RANK + IDS, LANES))],
        ),
        out_shape=[
            jax.ShapeDtypeStruct((KEYS, HALF), BF),
            jax.ShapeDtypeStruct((SHARDS, RANK + IDS, LANES), BF),
        ],
        compiler_params=params(56),
        cost_estimate=BRIEF,
        name="weight",
    )(idx, levels, scales, second, down, up, down, ids)


def grads_kernel(idx, everyone, own, rotated, freqs, up, grads, low):
    mine = own[...]
    count = jnp.zeros((ROWS, LANES), F32)
    for k in range(SHARDS):
        for r in range(2):
            row = everyone[k, r : r + 1, :].astype(F32)
            count = count + jnp.where(row < mine, 1.0, 0.0)
    first = jnp.sum(count, axis=1, keepdims=True)
    place = lax.broadcasted_iota(jnp.int32, (ROWS, 1), 0) + idx[3] * ROWS
    position = place.astype(F32) - first
    angle = position * freqs[...]
    cosine = jnp.cos(angle)
    lane = lax.broadcasted_iota(jnp.int32, (ROWS, HEAD), 1)
    sine = jnp.where(lane < HEAD // 2, 1.0, -1.0) * jnp.sin(angle)
    for h in range(KEYS // HEAD):
        cols = slice(h * HEAD, (h + 1) * HEAD)
        g = rotated[:, cols].astype(F32)
        grads[:, cols] = (g * cosine + pltpu.roll(g, HEAD // 2, 1) * sine).astype(BF)
    low[...] = dot(up[...], grads[...], 1, 1).astype(BF)


def make_grads(idx, everyone, own, rotated, freqs, up):
    full = lambda shape: pl.BlockSpec(shape, lambda i, s: (0,) * len(shape))
    return pl.pallas_call(
        grads_kernel,
        grid_spec=pltpu.PrefetchScalarGridSpec(
            num_scalar_prefetch=1,
            grid=(1,),
            in_specs=[
                pl.BlockSpec((SHARDS, IDS, LANES), lambda i, s: (0, RANK // IDS, 0)),
                full((ROWS, 1)),
                full((ROWS, KEYS)),
                full((1, HEAD)),
                full((RANK, KEYS)),
            ],
            out_specs=[full((ROWS, KEYS)), full((RANK, ROWS))],
        ),
        out_shape=[jax.ShapeDtypeStruct((ROWS, KEYS), BF), jax.ShapeDtypeStruct((RANK, ROWS), BF)],
        compiler_params=params(56),
        cost_estimate=BRIEF,
        name="grads",
    )(idx, everyone, own, rotated, freqs, up)


CHUNKS = 8
WIDE = WIDTH // CHUNKS
STEP = WIDE // (2 * HALF)


def down_kernel(idx, low, tokens, *refs):
    keep, send, (held, keep_held, send_held, sems) = refs[:2], refs[2:4], refs[4:]
    c, x = idx[0], idx[2]
    loads = [
        pltpu.make_async_copy(tokens.at[:, pl.ds(i * WIDE, WIDE)], held.at[i], sems.at[i]) for i in range(CHUNKS)
    ]
    for load in loads:
        load.start()
    stores = []
    for i in range(CHUNKS):
        loads[i].wait()
        for k in range(STEP):
            at = (i * STEP + k) * HALF
            mine = pl.multiple_of(k * 2 * HALF + c * HALF, HALF)
            other = pl.multiple_of(k * 2 * HALF + (1 - c) * HALF, HALF)
            send_held[:, at : at + HALF] = dot(low[...], held[i, :, pl.ds(other, HALF)], 1, 0).astype(BF)
            keep_held[:, at : at + HALF] = dot(low[...], held[i, :, pl.ds(mine, HALF)], 1, 0)
    for d in range(2):
        half = WIDTH // 4
        cols = pl.ds(pl.multiple_of(lax.rem(x + d, 2) * half, half), half)
        for source, target in ((send_held, send[d]), (keep_held, keep[d])):
            stores.append(pltpu.make_async_copy(source.at[:, cols], target, sems.at[CHUNKS + len(stores)]))
            stores[-1].start()
    for store in stores:
        store.wait()


def down_part(idx, low, tokens):
    anywhere = pl.BlockSpec(memory_space=pl.ANY)
    return pl.pallas_call(
        down_kernel,
        in_specs=[pl.BlockSpec(memory_space=pltpu.SMEM), pl.BlockSpec(memory_space=pltpu.VMEM), anywhere],
        out_specs=[anywhere] * 4,
        out_shape=[jax.ShapeDtypeStruct((RANK, WIDTH // 4), dtype) for dtype in (F32, F32, BF, BF)],
        scratch_shapes=[
            pltpu.VMEM((CHUNKS, ROWS, WIDE), BF),
            pltpu.VMEM((RANK, WIDTH // 2), F32),
            pltpu.VMEM((RANK, WIDTH // 2), BF),
            pltpu.SemaphoreType.DMA((CHUNKS + 4,)),
        ],
        compiler_params=params(56),
        cost_estimate=BRIEF,
        name="down",
    )(idx, low, tokens)


def up_kernel(idx, tokens, *refs):
    given, (grads, out, held, lows, sems) = refs[:2], refs[2:]
    c = idx[0]
    loads = [
        pltpu.make_async_copy(tokens.at[:, pl.ds(i * WIDE, WIDE)], held.at[i], sems.at[i]) for i in range(CHUNKS)
    ]
    pieces = [pltpu.make_async_copy(p, lows.at[k], sems.at[CHUNKS + k]) for k, p in enumerate(given)]
    for copy in pieces + loads:
        copy.start()
    for copy in pieces:
        copy.wait()
    total = jnp.zeros((ROWS, RANK), F32)
    for i in range(CHUNKS):
        loads[i].wait()
        for k in range(STEP):
            for p in range(2):
                h = c if p == 0 else 1 - c
                at = pl.multiple_of(k * 2 * HALF + h * HALF, HALF)
                rows = jnp.concatenate([lows[p, q, i * STEP + k] for q in range(4)], axis=1)
                total = total + dot(held[i, :, pl.ds(at, HALF)], rows, 1, 1)
    product = dot(total.astype(BF), grads[...], 0, 0).astype(BF)
    for k in range(8):
        half = (k // 2) % 2 * (KEYS // 2)
        out[k] = product[:, half : half + KEYS // 2]


def up_part(idx, tokens, lows, grads):
    anywhere = pl.BlockSpec(memory_space=pl.ANY)
    return pl.pallas_call(
        up_kernel,
        in_specs=[pl.BlockSpec(memory_space=pltpu.SMEM)]
        + [anywhere] * 3
        + [pl.BlockSpec(memory_space=pltpu.VMEM)],
        out_specs=pl.BlockSpec(memory_space=pltpu.VMEM),
        out_shape=jax.ShapeDtypeStruct((8, RANK, KEYS // 2), BF),
        scratch_shapes=[
            pltpu.VMEM((CHUNKS, ROWS, WIDE), BF),
            pltpu.VMEM((2, 4, SHARDS, RANK, LANES), BF),
            pltpu.SemaphoreType.DMA((CHUNKS + 2,)),
        ],
        compiler_params=params(56),
        cost_estimate=BRIEF,
        name="up",
    )(idx, tokens, *lows, grads)


def block_kernel(first, second, weight, after, o0, o1, rows, held, made, sems):
    loads = [
        pltpu.make_async_copy(weight.at[pl.ds(i * KEYS, KEYS), :], held.at[i], sems.at[2 * NZ + i]) for i in range(NZ)
    ]
    for load in loads:
        load.start()
    rows[:ROWS, :] = first[...]
    rows[ROWS:, :] = second[...]
    stores = []
    for i in range(NZ):
        loads[i].wait()
        made[i] = dot(rows[...], held[i], 1, 0).astype(BF)
        for k, out in enumerate((o0, o1)):
            stores.append(
                pltpu.make_async_copy(
                    made.at[i, pl.ds(k * ROWS, ROWS), :],
                    out.at[:, pl.ds(i * HALF, HALF)],
                    sems.at[2 * i + k],
                )
            )
            stores[-1].start()
    for store in stores:
        store.wait()


def blocks(sources, weight, after):
    anywhere = pl.BlockSpec(memory_space=pl.ANY)
    return pl.pallas_call(
        block_kernel,
        in_specs=[pl.BlockSpec(memory_space=pltpu.VMEM)] * 2 + [anywhere] * 2,
        out_specs=[anywhere] * 2,
        out_shape=[jax.ShapeDtypeStruct((ROWS, NZ * HALF), BF)] * 2,
        scratch_shapes=[
            pltpu.VMEM((2 * ROWS, KEYS), BF),
            pltpu.VMEM((NZ, KEYS, HALF), BF),
            pltpu.VMEM((NZ, 2 * ROWS, HALF), BF),
            pltpu.SemaphoreType.DMA((3 * NZ,)),
        ],
        compiler_params=params(56),
        cost_estimate=BRIEF,
        name="blocks",
    )(*sources, weight, after)


def assemble_kernel(places, idx, *refs):
    out, sems = refs[-2:]
    copies = []
    for k, piece in zip(places, refs):
        x = idx[2] if k < 2 else 1 - idx[2]
        h = idx[0] if k % 2 == 0 else 1 - idx[0]
        for j in range(NZ):
            col = pl.multiple_of(((x * NZ + j) * 2 + h) * HALF, HALF)
            copies.append(
                pltpu.make_async_copy(
                    piece.at[:, pl.ds(j * HALF, HALF)],
                    out.at[:, pl.ds(col, HALF)],
                    sems.at[len(copies)],
                )
            )
    for copy in copies:
        copy.start()
    for copy in copies:
        copy.wait()


def assemble(idx, places, pieces, before):
    anywhere = pl.BlockSpec(memory_space=pl.ANY)
    return pl.pallas_call(
        functools.partial(assemble_kernel, places),
        in_specs=[pl.BlockSpec(memory_space=pltpu.SMEM)]
        + [pl.BlockSpec(memory_space=pltpu.VMEM)] * len(pieces)
        + [anywhere] * len(before),
        out_specs=anywhere,
        scratch_shapes=[pltpu.SemaphoreType.DMA((NZ * len(pieces),))],
        out_shape=jax.ShapeDtypeStruct((ROWS, WIDTH), BF),
        input_output_aliases={1 + len(pieces): 0} if before else {},
        compiler_params=params(8),
        cost_estimate=BRIEF,
        name="assemble",
    )(idx, *pieces, *before)


def x_permutation(swap):
    at = lambda x, c: ((x // 2) * 2 + c) * 2 + x % 2
    pairs = []
    for x in range(4):
        for c in range(2):
            if (c ^ swap) == 0:
                pairs.append((at(x, c), at((x + 1) % 4, 0)))
            else:
                pairs.append((at(x, c), at((x - 1) % 4, 1)))
    return pairs


def inverse(pairs):
    return [(b, a) for a, b in pairs]


CORE = [(0, 1), (1, 0)]


def on_device(tokens, rotated, documents, levels, scales, second, down, up):
    xh, y, c, xl, z = (lax.axis_index(a) for a in ("xh", "y", "c", "xl", "z"))
    idx = jnp.stack([c, xh, xl, xl * NZ + z, y]).astype(jnp.int32)

    ids = jnp.pad(documents, ((0, 0), (0, 2 * LANES - ROWS)), constant_values=1000)
    weight, packet = local_weight(idx, levels, scales, second, down.T, up, ids)
    weight = lax.all_gather(weight, "z", tiled=True)
    everyone = lax.all_to_all(packet, SHARD_AXES, 0, 0, tiled=True)

    half = HEAD // 2
    freqs = ROPE_BASE ** (-jnp.arange(half, dtype=F32) * 2.0 / HEAD)
    freqs = jnp.concatenate([freqs, freqs])[None, :]
    own = documents.astype(F32).reshape(ROWS, 1)
    grads, low = make_grads(idx, everyone, own, rotated, freqs, up)

    there, across = x_permutation(0), x_permutation(1)
    sources = [
        grads,
        lax.ppermute(grads, "c", CORE),
        lax.ppermute(grads, X_AXES, there),
        lax.ppermute(grads, X_AXES, across),
    ]

    made = down_part(idx, low, tokens)
    keep, send = made[:2], made[2:]
    sent = [lax.ppermute(part, "c", CORE) for part in send]

    lows = jnp.broadcast_to(everyone[None, :, :RANK], (4, SHARDS, RANK, LANES))
    lows = lax.all_to_all(lows, "y", 0, 0, tiled=True)
    lows, sent = lax.optimization_barrier((lows, sent))
    lows = [lows, lax.ppermute(lows, "c", CORE)]

    halves = [(a + b.astype(F32)).reshape(2, RANK // 2, WIDTH // 4) for a, b in zip(keep, sent)]
    own_half = lax.dynamic_index_in_dim(halves[0], xh, 0, keepdims=False)
    parcels = [
        lax.dynamic_index_in_dim(half, at, 0, keepdims=False).astype(BF)
        for half, at in ((halves[0], 1 - xh), (halves[1], xh), (halves[1], 1 - xh))
    ]
    parcels, sources[1:] = lax.optimization_barrier((parcels, sources[1:]))
    parcels = [
        lax.ppermute(parcel, ("xh", "xl"), [(i, i ^ bits) for i in range(4)])
        for parcel, bits in zip(parcels, (2, 1, 3))
    ]

    up_total = up_part(idx, tokens, lows, grads)
    away = blocks(sources[2:], weight, up_total)
    here = blocks(sources[:2], weight, away[0])
    pieces = [
        here[0],
        lax.ppermute(here[1], "c", CORE),
        lax.ppermute(away[0], X_AXES, inverse(there)),
        lax.ppermute(away[1], X_AXES, inverse(across)),
    ]

    up_total = lax.all_to_all(up_total, X_AXES, 0, 0, tiled=True)
    parcels, up_total, _ = lax.optimization_barrier((parcels, up_total, away[0]))
    up_total = jnp.sum(up_total.astype(F32), axis=0).reshape(4, RANK // 8, KEYS)
    total = own_half + parcels[0].astype(F32) + parcels[1].astype(F32) + parcels[2].astype(F32)
    total = jnp.concatenate([total.reshape(4, RANK // 8, WIDTH // 4), up_total], axis=2)
    mine = lax.dynamic_index_in_dim(total, y, 0, keepdims=False)
    for d in (1, 3, 2):
        out = lax.dynamic_index_in_dim(total, (y + d) % 4, 0, keepdims=False).astype(BF)
        mine = mine + lax.ppermute(out, "y", [(i, (i + d) % 4) for i in range(4)]).astype(F32)
    total = mine.astype(BF)

    slabs = total[:, : WIDTH // 4].reshape(RANK // 8, NZ, HALF).transpose(1, 0, 2)
    up_total = jnp.broadcast_to(total[None, :, WIDTH // 4 :], (NZ, RANK // 8, KEYS))
    slabs = jnp.concatenate([slabs, up_total], axis=1)
    slabs, pieces[0] = lax.optimization_barrier((slabs, pieces[0]))
    slabs = lax.all_to_all(slabs, "z", 0, 0, tiled=True)
    slabs = jnp.sum(slabs.astype(F32), axis=0).astype(BF)
    slabs, pieces[2] = lax.optimization_barrier((slabs, pieces[2]))
    slabs = jnp.broadcast_to(slabs[None], (16,) + slabs.shape)
    slabs = lax.all_to_all(slabs, DP_AXES, 0, 0, tiled=True).astype(F32)
    factor = SCALE / jnp.sqrt(jnp.float32(TOKENS))
    slabs = factor * slabs.reshape(2, 4, 2, RANK // 4, KEYS)
    grad_down = slabs[:, :, :, : RANK // 8].transpose(2, 4, 0, 1, 3).reshape(2 * HALF, RANK)
    grad_up = slabs[0, :, :, RANK // 8 :].reshape(4, 2, RANK // 4, KEYS // 2)
    grad_up = grad_up.transpose(0, 2, 1, 3).reshape(RANK, KEYS)

    grad_tokens = assemble(idx, (0, 1, 2), pieces[:3], [])
    grad_tokens = assemble(idx, (3,), pieces[3:], [grad_tokens])
    return grad_tokens, grad_down, grad_up


def solution(mesh):
    fine = Mesh(mesh.devices.reshape(2, 4, 2, 2, 8), ("xh", "y", "c", "xl", "z"))
    everything = DP_AXES + SHARD_AXES
    in_specs = (
        P(everything, None),
        P(everything, None),
        P(DP_AXES, SHARD_AXES),
        P(SHARD_AXES, None),
        P(SHARD_AXES, None),
        P(),
        P(SHARD_AXES, None),
        P(),
    )
    out_specs = (P(everything, None), P(SHARD_AXES, None), P())
    return jax.shard_map(on_device, mesh=fine, in_specs=in_specs, out_specs=out_specs, check_vma=False)
```
